128 devices in a mesh: gz: 32 (over y, x, core), gy: 4 (over z).
Axes of the slice: x: 4, y: 4, z: 4, core: 2. Of those that a mesh axis runs over, the one named last changes fastest.
Arguments:
- volume: float32 [512, 512, 512], P('gz', 'gy'), may hold values from -6 to 6
- labels: int32 [512, 512, 512], P('gz', 'gy'), may hold values from 0 to 3
- patch_list: int32 [32, 4, 256], P('gz', 'gy'), may hold values from -1 to 255, as said below
- stem_kernel: float32 [3, 3, 3], replicated, may hold values from -1.25 to 1.25
- embed_weight: bfloat16 [4096, 1024], replicated, may hold values from -0.09375 to 0.09375
- norm_gain: float32 [2, 1024], replicated, may hold values from 0.1 to 1.9
- up_weight: bfloat16 [2, 1024, 4096], P(None, None, 'gy'), may hold values from -0.1875 to 0.1875
- down_weight: bfloat16 [2, 4096, 1024], P(None, 'gy'), may hold values from -0.09375 to 0.09375
- head_weight: bfloat16 [1024, 256], replicated, may hold values from -0.1875 to 0.1875
- skip_weight: float32 [4], replicated, may hold values from -3 to 3
- class_bias: float32 [4], replicated, may hold values from -3 to 3
Outputs:
- patch_dice: float32 [32, 4, 4, 256], P('gz', 'gy')
- dice: float32 [4], replicated
The draws below stay inside these ranges and needn't reach their ends.
Inputs may be any that keep to these rules, and one draw needn't show every extreme that they name: `patch_list`: each device block's row lists the numbers of its listed patches, each once and ascending, followed by -1 in the remaining slots; over all blocks exactly 20480 patches are listed, and some block lists all 256 of its patches.
All inputs are finite; a program needn't handle non-finite values.
Results may differ from the reference program's by a relative error of at most 0.0008.
Values may be sent and summed in bfloat16 or wider, within the bound.
A program may use at most 256 MiB of HBM per device.

```python
import jax
import jax.numpy as jnp
from jax import lax

D = 1024
HID = 4096
PS = 16
ROW_DEV = 128
COLS = 512
LAYERS = 2
CLASSES = 4
VOX = 4096
HEAD = 256
PATCH_DEV = 256
KEEP = 160
TOTAL = 20480
NX = 512
NY = 512
NZ = 512
N_GZ = 32
N_GY = 4


def draw_labels(key, part):
    key = jax.random.fold_in(key, 7)
    depth = jnp.arange(NX, dtype=jnp.int32) * 1000 // NX
    first = 400 - depth // 4
    second = first + 100 + depth // 4
    third = second + 300 - depth // 5
    picks = jax.random.randint(key, (NX, NY, NZ), 0, 1000, dtype=jnp.int32)
    result = (picks >= first[:, None, None]).astype(jnp.int32)
    result = result + (picks >= second[:, None, None]).astype(jnp.int32)
    result = result + (picks >= third[:, None, None]).astype(jnp.int32)
    return result


def draw_patch_list(key, part):
    key = jax.random.fold_in(key, 11)
    devices = N_GZ * N_GY
    key_order, key_pair, key_score = jax.random.split(key, 3)
    order = jax.random.permutation(key_order, devices).astype(jnp.int32)
    pair_count = jax.random.randint(key_pair, (devices // 2,), 2 * KEEP - PATCH_DEV, PATCH_DEV + 1, dtype=jnp.int32)
    pair_count = pair_count.at[0].set(PATCH_DEV)
    paired = jnp.stack([pair_count, 2 * KEEP - pair_count], 1).reshape(devices)
    counts = jnp.zeros((devices,), jnp.int32).at[order].set(paired)
    position = jnp.arange(PATCH_DEV, dtype=jnp.int32)
    scores = jax.random.randint(key_score, (devices, PATCH_DEV), 0, 1 << 20, dtype=jnp.int32) * PATCH_DEV + position[None, :]
    ranking = jnp.argsort(jnp.argsort(scores, axis=1), axis=1).astype(jnp.int32)
    chosen = ranking < counts[:, None]
    listing = jnp.sort(jnp.where(chosen, position[None, :], PATCH_DEV), axis=1)
    listing = jnp.where(listing == PATCH_DEV, -1, listing).astype(jnp.int32)
    return listing.reshape(N_GZ, N_GY, PATCH_DEV)


def block_scale(key, shape, cuts, least, high):
    loudness, own = 1.0, jax.random.fold_in(key, 6)
    for axis_at, parts in cuts:
        steps = jnp.exp(jax.random.uniform(jax.random.fold_in(own, axis_at), (parts,), jnp.float32, least / len(cuts), high / len(cuts)))
        loudness = loudness * jnp.repeat(steps, shape[axis_at] // parts).reshape([-1 if axis == axis_at else 1 for axis in range(len(shape))])
    return loudness


def scatter_about(rng, dims, scale, reach, cuts=(), kind=jnp.bfloat16):
    entries = scale * jax.random.normal(rng, dims, jnp.float32)
    if cuts:
        entries = entries * block_scale(rng, dims, cuts, -0.22, 0.18)
    return jnp.clip(entries, -reach, reach).astype(kind)


def setup_inputs(seed: int = 0) -> dict:
    arg_keys = jax.random.split(jax.random.key(seed), 12)
    return {
        "volume": scatter_about(arg_keys[0], (NX, NY, NZ), 1.0, 6.0, ((0, 32), (1, 4)), jnp.float32),
        "labels": draw_labels(jax.random.fold_in(arg_keys[11], 71), 0),
        "patch_list": draw_patch_list(jax.random.fold_in(arg_keys[11], 71), 0),
        "stem_kernel": scatter_about(arg_keys[3], (3, 3, 3), 27 ** -0.5, 1.25, (), jnp.float32),
        "embed_weight": scatter_about(arg_keys[4], (VOX, D), VOX ** -0.5, 0.09375),
        "norm_gain": jnp.clip(1.0 + 0.18 * jax.random.normal(arg_keys[5], (LAYERS, D), jnp.float32), 0.1, 1.9),
        "up_weight": scatter_about(arg_keys[6], (LAYERS, D, HID), D ** -0.5, 0.1875, ((2, 4),)),
        "down_weight": scatter_about(arg_keys[7], (LAYERS, HID, D), HID ** -0.5, 0.09375, ((1, 4),)),
        "head_weight": scatter_about(arg_keys[8], (D, HEAD), D ** -0.5, 0.1875),
        "skip_weight": scatter_about(arg_keys[9], (CLASSES,), 1.0, 3.0, (), jnp.float32),
        "class_bias": scatter_about(arg_keys[10], (CLASSES,), 1.0, 3.0, (), jnp.float32),
    }


EPS = 1e-05

def stem_field(volume, stem_kernel):
    depth, rows, cols = volume.shape
    padded = jnp.pad(volume, 1)
    total = jnp.zeros(volume.shape, jnp.float32)
    for first in range(3):
        for second in range(3):
            for third in range(3):
                total = total + stem_kernel[first, second, third] * padded[first:first + depth, second:second + rows, third:third + cols]
    return jax.nn.silu(total).astype(jnp.bfloat16)

def patch_layout(field):
    blocks_r = ROW_DEV // PS
    blocks_c = COLS // PS
    shaped = field.reshape(N_GZ, PS, N_GY, blocks_r, PS, blocks_c, PS)
    return shaped.transpose(0, 2, 3, 5, 1, 4, 6).reshape(N_GZ, N_GY, blocks_r * blocks_c, PS * PS * PS)

def normalize(rows, gain):
    values = rows.astype(jnp.float32)
    centre = lax.optimization_barrier(jnp.mean(values, -1, keepdims=True))
    centred = values - centre
    spread = lax.optimization_barrier(jnp.mean(centred * centred, -1, keepdims=True))
    return (centred * lax.rsqrt(spread + EPS) * gain).astype(jnp.bfloat16)

def mlp_layer(tokens, gain, up_matrix, down_matrix):
    normed = normalize(tokens, gain)
    share = up_matrix.shape[1] // N_GY
    total = jnp.zeros(tokens.shape, jnp.float32)
    for index in range(N_GY):
        upper = jnp.dot(normed, up_matrix[:, index * share:(index + 1) * share], preferred_element_type=jnp.float32)
        active = jax.nn.gelu(upper, approximate=True).astype(jnp.bfloat16)
        part = jnp.dot(active, down_matrix[index * share:(index + 1) * share], preferred_element_type=jnp.float32)
        total = total + lax.optimization_barrier(part.astype(jnp.bfloat16)).astype(jnp.float32)
    return (tokens.astype(jnp.float32) + total).astype(jnp.bfloat16)

def expand_blocks(coarse):
    lead = coarse.shape[:-1]
    edge = PS // 4
    grid = coarse.reshape(lead + (CLASSES, 4, 1, 4, 1, 4, 1))
    grid = jnp.broadcast_to(grid, lead + (CLASSES, 4, edge, 4, edge, 4, edge))
    return grid.reshape(lead + (CLASSES, 64 * edge * edge * edge))

def patch_terms(coarse_vox, stem_rows, label_rows, skip_weight, class_bias):
    logits = coarse_vox + skip_weight[:, None] * stem_rows.astype(jnp.float32)[..., None, :] + class_bias[:, None]
    probs = jax.nn.sigmoid(logits)
    classes = jnp.arange(CLASSES, dtype=jnp.int32)
    match = (label_rows[..., None, :] == classes[:, None]).astype(jnp.float32)
    return (lax.optimization_barrier(jnp.sum(probs * match, -1)), lax.optimization_barrier(jnp.sum(probs, -1)), lax.optimization_barrier(jnp.sum(match, -1)))

def reference(volume, labels, patch_list, stem_kernel, embed_weight, norm_gain, up_weight, down_weight, head_weight, skip_weight, class_bias):
    stem = stem_field(volume, stem_kernel)
    stem_rows = patch_layout(stem)
    label_rows = patch_layout(labels)
    flat_rows = stem_rows.reshape(N_GZ * N_GY * PATCH_DEV, VOX)
    flat_list = patch_list.reshape(N_GZ * N_GY, PATCH_DEV)
    starts = jnp.arange(N_GZ * N_GY, dtype=jnp.int32)[:, None] * PATCH_DEV
    global_ids = (starts + jnp.maximum(flat_list, 0)).reshape(-1).astype(jnp.int32)
    listed = (flat_list >= 0).reshape(-1)
    picks = jnp.nonzero(listed, size=TOTAL)[0].astype(jnp.int32)
    targets = global_ids[picks]
    tokens = jnp.dot(flat_rows[targets], embed_weight, preferred_element_type=jnp.float32).astype(jnp.bfloat16)
    for layer in range(LAYERS):
        tokens = mlp_layer(tokens, norm_gain[layer], up_weight[layer], down_weight[layer])
    coarse = jnp.dot(tokens, head_weight, preferred_element_type=jnp.float32).astype(jnp.bfloat16)
    table = jnp.zeros((N_GZ * N_GY * PATCH_DEV, HEAD), jnp.float32).at[targets].set(coarse.astype(jnp.float32))
    table = table.reshape(N_GZ, N_GY, PATCH_DEV, HEAD)

    def slab(items):
        coarse_slab, stem_slab, label_slab = items
        return patch_terms(expand_blocks(coarse_slab), stem_slab, label_slab, skip_weight, class_bias)
    inter, mass, count = lax.map(slab, (table, stem_rows, label_rows))
    patch_dice = ((2.0 * inter + 1.0) / (mass + count + 1.0)).transpose(0, 1, 3, 2)
    dice = (2.0 * lax.optimization_barrier(jnp.sum(inter, (0, 1, 2))) + 1.0) / (lax.optimization_barrier(jnp.sum(mass, (0, 1, 2))) + lax.optimization_barrier(jnp.sum(count, (0, 1, 2))) + 1.0)
    return (patch_dice, dice)
```

```python
import jax
import jax.numpy as jnp
from jax import lax
from jax.experimental import pallas as pl
from jax.experimental.pallas import tpu as pltpu
from jax.sharding import PartitionSpec as P

EPS = 1e-05
MESH = pl.DeviceIdType.MESH
F32 = jnp.float32
BF16 = jnp.bfloat16

NEAR, FAR, HALF = 128, 512, 64


def kernel(
    vol, lab, slots, taps, emb, gain, up, down, head, skip, bias,
    out,
    pad, wts, embuf, stem, labels, lhs, xacc, xn, hid, coarse, upq, expand, sums, headbuf, gainbuf,
    hs, hr, cs, cr, vsem, labsem, z1s, z1r, z2s, z2r, a1s, a1r, a2s, a2r, ss, sr, lsem,
):
    gz, gy = lax.axis_index("gz"), lax.axis_index("gy")
    core = lax.rem(gz, 2)
    chip = lax.div(gz, 2)
    cx, cy = lax.rem(chip, 4), lax.div(chip, 4)
    seed = (1 - core) * cx + core * cy

    def along(step):
        first = (cy * 4 + lax.rem(cx + step, 4)) * 2
        second = (lax.rem(cy + step, 4) * 4 + cx) * 2 + 1
        return ((1 - core) * first + core * second, gy)

    z_next, z_prev = (gz, lax.rem(gy + 1, 4)), (gz, lax.rem(gy + 3, 4))
    a_next, a_prev = along(1), along(3)
    g_next, g_prev = (lax.rem(gz + 1, 32), gy), (lax.rem(gz + 31, 32), gy)
    twin = (gz + 1 - 2 * core, gy)
    q_prev, q_next, q_far = lax.rem(gy + 3, 4), lax.rem(gy + 1, 4), lax.rem(gy + 2, 4)
    foreign = (q_prev, q_next, q_far)

    barrier = pltpu.get_barrier_semaphore()
    for peer in (z_next, z_prev, a_next, a_prev, g_next, g_prev, twin):
        pl.semaphore_signal(barrier, inc=1, device_id=peer, device_id_type=MESH)
    pl.semaphore_wait(barrier, 7)

    def remote(src, dst, send, recv, peer):
        return pltpu.make_async_remote_copy(
            src_ref=src, dst_ref=dst, send_sem=send, recv_sem=recv, device_id=peer, device_id_type=MESH
        )

    sent = []

    def send(*args):
        copy = remote(*args)
        copy.start()
        sent.append(copy)

    def landed(dst, send_sem, recv_sem, peer):
        remote(dst, dst, send_sem, recv_sem, peer).wait_recv()

    body = pl.ds(8, 128)
    inner = pl.ds(1, 16)
    above, below = pl.ds(0, 8), pl.ds(136, 8)
    blocks = [pl.ds(cb * 128, 128) for cb in range(4)]
    for cb, cols in enumerate(blocks):
        send(vol.at[15, :, cols], pad.at[0, cb, body], hs.at[0, cb], hr.at[0, cb], g_next)
        send(vol.at[0, :, cols], pad.at[17, cb, body], hs.at[1, cb], hr.at[1, cb], g_prev)
    for cb, cols in enumerate(blocks):
        send(vol.at[:, pl.ds(120, 8), cols], pad.at[inner, cb, above], hs.at[2, cb], hr.at[2, cb], z_next)
        send(vol.at[:, pl.ds(0, 8), cols], pad.at[inner, cb, below], hs.at[3, cb], hr.at[3, cb], z_prev)

    groups = (4, 8, 12, 0)
    local = []
    parts = ((3, 6), (9, 4), (13, 3), (0, 3))
    for n, (first, many) in enumerate(parts):
        for cb, cols in enumerate(blocks):
            copy = pltpu.make_async_copy(
                vol.at[pl.ds(first, many), :, cols], pad.at[pl.ds(1 + first, many), cb, body], vsem.at[n, cb]
            )
            copy.start()
            local.append(copy)

    def volume_wait(n):
        for copy in local[n * 4 : n * 4 + 4]:
            copy.wait()

    def embed_copy(g):
        return pltpu.make_async_copy(
            emb.at[pl.ds(groups[g] * 256, 1024)], embuf.at[g % 2], lsem.at[4 + g % 2]
        )

    embed_copy(0).start()

    def own(t):
        return (up, down)[t % 2].at[t // 2]

    def rows(which, at, offset=0, size=NEAR):
        return pl.ds(which * FAR + at * NEAR + offset, size)

    def near(t, q, at):
        return wts.at[t // 2, t % 2, q, rows(core, at)]

    def half(t, q, at, h):
        return wts.at[t // 2, t % 2, q, rows(core, at, h * HALF, HALF)]

    seed_prev, seed_next, seed_far = lax.rem(seed + 3, 4), lax.rem(seed + 1, 4), lax.rem(seed + 2, 4)

    def step_z1(t):
        piece = own(t).at[rows(core, seed)]
        send(piece, near(t, gy, seed), z1s.at[t, 0], z1r.at[t, 0], z_next)
        send(piece, near(t, gy, seed), z1s.at[t, 1], z1r.at[t, 1], z_prev)

    def spread(t, n):
        piece = near(t, foreign[n], seed)
        send(piece, piece, a1s.at[t, n, 0], a1r.at[t, n, 0], a_next)
        send(piece, piece, a1s.at[t, n, 1], a1r.at[t, n, 1], a_prev)

    def step_b(t):
        landed(near(t, q_prev, seed), z1s.at[t, 0], z1r.at[t, 0], z_prev)
        piece = half(t, q_prev, seed, 0)
        send(piece, piece, z2s.at[t, 0], z2r.at[t, 0], z_next)
        spread(t, 0)
        landed(near(t, q_next, seed), z1s.at[t, 1], z1r.at[t, 1], z_next)
        piece = half(t, q_next, seed, 1)
        send(piece, piece, z2s.at[t, 1], z2r.at[t, 1], z_prev)
        spread(t, 1)

    def step_c(t):
        landed(half(t, q_far, seed, 0), z2s.at[t, 0], z2r.at[t, 0], z_prev)
        landed(half(t, q_far, seed, 1), z2s.at[t, 1], z2r.at[t, 1], z_next)
        spread(t, 2)

    def step_d(t, n):
        q = foreign[n]
        landed(near(t, q, seed_prev), a1s.at[t, n, 0], a1r.at[t, n, 0], a_prev)
        piece = half(t, q, seed_prev, 0)
        send(piece, piece, a2s.at[t, n, 0], a2r.at[t, n, 0], a_next)
        landed(near(t, q, seed_next), a1s.at[t, n, 1], a1r.at[t, n, 1], a_next)
        piece = half(t, q, seed_next, 1)
        send(piece, piece, a2s.at[t, n, 1], a2r.at[t, n, 1], a_prev)

    def step_e(t, n):
        q = foreign[n]
        landed(half(t, q, seed_far, 0), a2s.at[t, n, 0], a2r.at[t, n, 0], a_prev)
        landed(half(t, q, seed_far, 1), a2s.at[t, n, 1], a2r.at[t, n, 1], a_next)
        piece = wts.at[t // 2, t % 2, q, pl.ds(core * FAR, FAR)]
        send(piece, piece, ss.at[t, n], sr.at[t, n], twin)

    def step_f(t, n):
        dst = wts.at[t // 2, t % 2, foreign[n], pl.ds((1 - core) * FAR, FAR)]
        landed(dst, ss.at[t, n], sr.at[t, n], twin)

    order = [("z", 0), ("z", 1), ("b", 0), ("c", 0), ("z", 2), ("d", 0, 0), ("d", 0, 1), ("d", 0, 2)]
    order += [("b", 1), ("c", 1), ("e", 0, 0), ("e", 0, 1), ("e", 0, 2), ("z", 3)]
    order += [("d", 1, 0), ("d", 1, 1), ("d", 1, 2), ("b", 2), ("c", 2), ("f", 0, 0), ("f", 0, 1), ("f", 0, 2)]
    order += [("e", 1, 0), ("e", 1, 1), ("e", 1, 2), ("d", 2, 0), ("d", 2, 1), ("d", 2, 2), ("b", 3), ("c", 3)]
    order += [("f", 1, 0), ("f", 1, 1), ("f", 1, 2), ("e", 2, 0), ("e", 2, 1), ("e", 2, 2)]
    order += [("d", 3, 0), ("d", 3, 1), ("d", 3, 2), ("f", 2, 0), ("f", 2, 1), ("f", 2, 2)]
    order += [("e", 3, 0), ("e", 3, 1), ("e", 3, 2), ("f", 3, 0), ("f", 3, 1), ("f", 3, 2)]
    doing = {"z": step_z1, "b": step_b, "c": step_c, "d": step_d, "e": step_e, "f": step_f}

    def run_until(*last):
        while order:
            name, *args = order.pop(0)
            doing[name](*args)
            if (name, *args) == last:
                return

    run_until("z", 1)

    head_copy = pltpu.make_async_copy(head, headbuf, lsem.at[6])
    head_copy.start()
    gain_copy = pltpu.make_async_copy(gain, gainbuf, lsem.at[7])
    gain_copy.start()
    lab_copies = [
        pltpu.make_async_copy(lab.at[:, :, cols], labels.at[:, cb], labsem.at[cb]) for cb, cols in enumerate(blocks)
    ]
    mine = [
        pltpu.make_async_copy(own(t), wts.at[t // 2, t % 2, gy], lsem.at[9 + t]) for t in range(4)
    ]

    for cb in range(4):
        landed(pad.at[0, cb, body], hs.at[0, cb], hr.at[0, cb], g_prev)
        landed(pad.at[17, cb, body], hs.at[1, cb], hr.at[1, cb], g_next)
    corner = []
    for n, plane in enumerate((0, 17)):
        corner.append(remote(pad.at[plane, :, pl.ds(128, 8)], pad.at[plane, :, above], cs.at[n, 0], cr.at[n, 0], z_next))
        corner.append(remote(pad.at[plane, :, pl.ds(8, 8)], pad.at[plane, :, below], cs.at[n, 1], cr.at[n, 1], z_prev))
    for copy in corner:
        copy.start()
    for cb in range(4):
        landed(pad.at[inner, cb, above], hs.at[2, cb], hr.at[2, cb], z_prev)
        landed(pad.at[inner, cb, below], hs.at[3, cb], hr.at[3, cb], z_next)

    @pl.when(gy == 0)
    def _():
        pad[inner, :, above] = jnp.zeros((16, 4, 8, 128), F32)

    @pl.when(gy == 3)
    def _():
        pad[inner, :, below] = jnp.zeros((16, 4, 8, 128), F32)

    xacc[...] = jnp.zeros_like(xacc)
    lane = lax.broadcasted_iota(jnp.int32, (8, 512), 1)
    not_first, not_last = lane != 0, lane != 511
    block = lax.broadcasted_iota(jnp.int32, (8, 128), 1) // 16
    low = {bit: (block // bit) % 2 == 0 for bit in (1, 2, 4)}

    def stem_row(d, i):
        totals = [[], [], []]
        for cb in range(4):
            total = [None, None, None]
            for first in range(3):
                for second in range(3):
                    x = pad[d + first, cb, pl.ds(7 + i + second, 8, stride=16), :]
                    for third in range(3):
                        term = taps[(first * 3 + second) * 3 + third] * x
                        total[third] = term if total[third] is None else total[third] + term
            for third in range(3):
                totals[third].append(total[third])
        total = [jnp.concatenate(many, axis=1) for many in totals]
        left = jnp.where(not_first, pltpu.roll(total[0], 1, 1), 0.0)
        right = jnp.where(not_last, pltpu.roll(total[2], 511, 1), 0.0)
        v = 0.5 * (total[1] + left + right)
        v = v + v * jnp.tanh(v)
        stem[d, i] = v.astype(BF16).astype(F32)

    def stem_plane(d, at):
        @pl.loop(0, 16)
        def _(i):
            stem_row(d, i)

        for upper in range(2):
            for cb in range(4):
                v = [stem[d, upper * 8 + i, :, pl.ds(cb * 128, 128)] for i in range(8)]
                for bit in (1, 2, 4):
                    for i in range(8):
                        if i & bit == 0:
                            a, b = v[i], v[i + bit]
                            v[i] = jnp.where(low[bit], a, pltpu.roll(b, bit * 16, 1))
                            v[i + bit] = jnp.where(low[bit], pltpu.roll(a, 128 - bit * 16, 1), b)
                for m in range(4):
                    pair = jnp.concatenate([v[2 * m], v[2 * m + 1]], axis=0).astype(BF16)
                    lhs[at, pl.ds(cb * 64 + m * 16, 16), pl.ds(upper * 128, 128)] = pair

    def front(g):
        base = groups[g]

        @pl.loop(0, 4)
        def _(n):
            stem_plane(base + n, n)

        embed_copy(g).wait()
        slot = g % 2

        @pl.loop(0, 4)
        def _(n):
            cols = pl.ds(pl.multiple_of(n * 256, 256), 256)
            total = xacc[:, cols]
            for part in range(4):
                total = total + jnp.dot(
                    lhs[part], embuf[slot, pl.ds(part * 256, 256), cols], preferred_element_type=F32
                )
            xacc[:, cols] = total

    volume_wait(0)
    embed_copy(1).start()
    mine[0].start()
    mine[1].start()
    front(0)
    run_until("c", 0)
    volume_wait(1)
    embed_copy(2).start()
    front(1)
    run_until("d", 0, 2)
    for copy in corner:
        copy.wait()
    volume_wait(2)
    volume_wait(3)

    @pl.when(gz == 0)
    def _():
        pad[0] = jnp.zeros((4, 144, 128), F32)

    @pl.when(gz == 31)
    def _():
        pad[17] = jnp.zeros((4, 144, 128), F32)

    for plane in (0, 17):
        @pl.when(gy == 0)
        def _():
            pad[plane, :, above] = jnp.zeros((4, 8, 128), F32)

        @pl.when(gy == 3)
        def _():
            pad[plane, :, below] = jnp.zeros((4, 8, 128), F32)

    embed_copy(3).start()
    mine[2].start()
    mine[3].start()
    for copy in lab_copies:
        copy.start()
    front(2)
    run_until("e", 0, 2)
    front(3)
    run_until("c", 2)
    gain_copy.wait()
    for t in range(4):
        mine[t].wait()

    at_row = lax.broadcasted_iota(jnp.int32, (256, 512), 0) // 8
    at_col = lax.broadcasted_iota(jnp.int32, (256, 512), 1)
    for e in range(4):
        hit = jnp.logical_and(at_col // 16 == at_row, (at_col // 4) % 4 == e)
        expand[pl.ds(e * 256, 256)] = hit.astype(F32).astype(BF16)

    def as_stored(x):
        return x.astype(BF16).astype(F32)

    @pl.loop(0, 8)
    def _(n):
        at = pl.ds(pl.multiple_of(n * 32, 32), 32)
        xacc[at] = as_stored(xacc[at])

    def mlp_up(layer, q):
        @pl.loop(0, 4)
        def _(n):
            cols = pl.ds(pl.multiple_of(n * 256, 256), 256)
            u = jnp.dot(xn[...], wts[layer, 0, q, :, cols], preferred_element_type=F32)
            hid[q, :, cols] = jax.nn.gelu(u, approximate=True).astype(BF16)

    def mlp_down(layer, q):
        @pl.loop(0, 4)
        def _(n):
            cols = pl.ds(pl.multiple_of(n * 256, 256), 256)
            xacc[:, cols] += jnp.dot(hid[q], wts[layer, 1, q, :, cols], preferred_element_type=F32)

    for layer in range(2):
        @pl.loop(0, 8)
        def _(n):
            at = pl.ds(pl.multiple_of(n * 32, 32), 32)
            x = xacc[at]
            centred = x - jnp.mean(x, -1, keepdims=True)
            spread_ = jnp.mean(centred * centred, -1, keepdims=True)
            xn[at] = (centred * lax.rsqrt(spread_ + EPS) * gainbuf[pl.ds(layer, 1)]).astype(BF16)

        mlp_up(layer, gy)
        for n in range(3):
            run_until("f", 2 * layer, n)
            mlp_up(layer, foreign[n])
        mlp_down(layer, gy)
        for n in range(3):
            run_until("f", 2 * layer + 1, n)
            mlp_down(layer, foreign[n])

        @pl.loop(0, 8)
        def _(n):
            at = pl.ds(pl.multiple_of(n * 32, 32), 32)
            xacc[at] = as_stored(xacc[at])

    head_copy.wait()
    token = lax.broadcasted_iota(jnp.int32, (256, 256), 0)
    patch = (token % 8) * 32 + token // 8
    listed = jnp.max((slots[...] == patch).astype(F32), axis=1, keepdims=True)
    q = jnp.dot(xacc[...].astype(BF16), headbuf[...], preferred_element_type=F32)
    q = (as_stored(q) * listed).T
    coarse[0] = q[:, :128]
    coarse[1] = q[:, 128:]
    token = lax.broadcasted_iota(jnp.int32, (8, 256), 1)
    own_row = (token % 8 == lax.broadcasted_iota(jnp.int32, (8, 256), 0)).astype(F32)

    for c in range(4):
        spread_q = []
        for e in range(4):
            at = pl.ds(c * 64 + e, 16, stride=4)
            part = jnp.concatenate([coarse[0, at, :], coarse[1, at, :]], axis=1)
            spread_q.append((part[:, None, :] * own_row[None]).reshape(128, 256).astype(BF16))
        u = jnp.zeros((128, 512), F32)
        for e in range(4):
            u = u + jnp.dot(spread_q[e], expand[pl.ds(e * 256, 256)], preferred_element_type=F32)
        upq[pl.ds(c * 128, 128)] = 0.5 * (u + bias[c])
    for copy in lab_copies:
        copy.wait()

    half_skip = [0.5 * skip[c] for c in range(4)]
    for cb in range(4):
        cols = pl.ds(cb * 128, 128)

        def block_step(ab, carry):
            carry = list(carry)
            a, b = lax.div(ab, 4), lax.rem(ab, 4)
            level = [upq[pl.ds(pl.multiple_of(c * 128 + ab * 8, 8), 8), cols] for c in range(4)]
            for dd in range(4):
                for ii in range(4):
                    d, i = a * 4 + dd, b * 4 + ii
                    s = stem[d, i, :, cols]
                    l = labels[d, cb, pl.ds(i, 8, stride=16), :]
                    for c in range(4):
                        t = jnp.tanh(level[c] + half_skip[c] * s)
                        carry[c] = carry[c] + t
                        match = l == c
                        carry[4 + c] = carry[4 + c] + jnp.where(match, t, 0.0)
                        carry[8 + c] = carry[8 + c] + jnp.where(match, 1.0, 0.0)
            return tuple(carry)

        final = lax.fori_loop(0, 16, block_step, (jnp.zeros((8, 128), F32),) * 12)
        for c in range(4):
            sums[pl.ds(c * 8, 8), cols] = 0.5 * (final[4 + c] + final[8 + c])
            sums[pl.ds(32 + c * 8, 8), cols] = 8 * 16 + 0.5 * final[c]
            sums[pl.ds(64 + c * 8, 8), cols] = final[8 + c]

    fold = lax.broadcasted_iota(jnp.int32, (512, 128), 0) // 16 == lax.broadcasted_iota(jnp.int32, (512, 128), 1)
    out[...] = jnp.dot(
        sums[...], fold.astype(F32), preferred_element_type=F32, precision=lax.Precision.HIGHEST
    )

    for copy in sent:
        copy.wait_send()


def per_device(
    volume, labels, patch_list, stem_kernel, embed_weight, norm_gain, up_weight, down_weight, head_weight, skip_weight, class_bias
):
    hbm = pl.BlockSpec(memory_space=pl.ANY)
    smem = pl.BlockSpec(memory_space=pltpu.SMEM)
    vmem = pl.BlockSpec(memory_space=pltpu.VMEM)
    dma = pltpu.SemaphoreType.DMA
    raw = pl.pallas_call(
        kernel,
        out_shape=jax.ShapeDtypeStruct((96, 128), F32),
        in_specs=[hbm, hbm, vmem, smem, hbm, hbm, hbm, hbm, hbm, smem, smem],
        out_specs=vmem,
        scratch_shapes=[
            pltpu.VMEM((18, 4, 144, 128), F32),
            pltpu.VMEM((2, 2, 4, 1024, 1024), BF16),
            pltpu.VMEM((2, 1024, 1024), BF16),
            pltpu.VMEM((16, 16, 8, 512), F32),
            pltpu.VMEM((16, 4, 128, 128), jnp.int32),
            pltpu.VMEM((4, 256, 256), BF16),
            pltpu.VMEM((256, 1024), F32),
            pltpu.VMEM((256, 1024), BF16),
            pltpu.VMEM((4, 256, 1024), BF16),
            pltpu.VMEM((2, 256, 128), F32),
            pltpu.VMEM((512, 512), F32),
            pltpu.VMEM((1024, 512), BF16),
            pltpu.VMEM((96, 512), F32),
            pltpu.VMEM((1024, 256), BF16),
            pltpu.VMEM((2, 1024), F32),
            dma((4, 4)), dma((4, 4)), dma((2, 2)), dma((2, 2)), dma((4, 4)), dma((4,)),
            dma((4, 2)), dma((4, 2)), dma((4, 2)), dma((4, 2)),
            dma((4, 3, 2)), dma((4, 3, 2)), dma((4, 3, 2)), dma((4, 3, 2)),
            dma((4, 3)), dma((4, 3)),
            dma((13,)),
        ],
        compiler_params=pltpu.CompilerParams(
            collective_id=0, has_side_effects=True, vmem_limit_bytes=60 * 1024 * 1024
        ),
    )(
        volume, labels, patch_list.reshape(1, 256), stem_kernel.reshape(27), embed_weight, norm_gain,
        up_weight, down_weight, head_weight, skip_weight, class_bias,
    )
    parts = raw[:, :32].reshape(3, 4, 256)
    inter, mass, count = parts[0], parts[1], parts[2]
    patch_dice = ((2.0 * inter + 1.0) / (mass + count + 1.0))[None, None]
    totals = lax.psum(jnp.sum(parts, 2), ("gz", "gy"))
    dice = (2.0 * totals[0] + 1.0) / (totals[1] + totals[2] + 1.0)
    return (patch_dice, dice)


def solution(mesh):
    placed = (
        P("gz", "gy", None),
        P("gz", "gy", None),
        P("gz", "gy", None),
        P(),
        P(),
        P(),
        P(None, None, "gy"),
        P(None, "gy", None),
        P(),
        P(),
        P(),
    )
    return jax.shard_map(
        per_device,
        mesh=mesh,
        in_specs=placed,
        out_specs=(P("gz", "gy", None, None), P()),
        check_vma=False,
    )
```

```python
import itertools

import jax
import jax.numpy as jnp
from jax import lax
from jax.experimental import pallas as pl
from jax.experimental.pallas import tpu as pltpu
from jax.sharding import PartitionSpec as P

EPS = 1e-05
MESH = pl.DeviceIdType.MESH
F32 = jnp.float32
BF16 = jnp.bfloat16

NEAR, FAR, HALF = 128, 512, 64


def kernel(
    vol, lab, slots, taps, emb, gain, up, down, head, skip, bias,
    out, dice,
    pad, wts, embuf, stem, labels, lhs, xacc, xn, hid, coarse, upq, expand, sums, headbuf, gainbuf, inbox, outbox,
    hs, hr, cs, cr, vsem, labsem, z1s, z1r, z2s, z2r, a1s, a1r, a2s, a2r, ss, sr, ps, pr, lsem,
):
    gz, gy = lax.axis_index("gz"), lax.axis_index("gy")
    core = lax.rem(gz, 2)
    chip = lax.div(gz, 2)
    cx, cy = lax.rem(chip, 4), lax.div(chip, 4)
    seed = (1 - core) * cx + core * cy

    def along(step):
        first = (cy * 4 + lax.rem(cx + step, 4)) * 2
        second = (lax.rem(cy + step, 4) * 4 + cx) * 2 + 1
        return ((1 - core) * first + core * second, gy)

    z_next, z_prev = (gz, lax.rem(gy + 1, 4)), (gz, lax.rem(gy + 3, 4))
    a_next, a_prev = along(1), along(3)
    g_next, g_prev = (lax.rem(gz + 1, 32), gy), (lax.rem(gz + 31, 32), gy)
    twin = (gz + 1 - 2 * core, gy)
    q_prev, q_next, q_far = lax.rem(gy + 3, 4), lax.rem(gy + 1, 4), lax.rem(gy + 2, 4)
    foreign = (q_prev, q_next, q_far)

    inner_group = [(n, (chip * 2 + lax.rem(core + n // 4, 2), lax.rem(gy + n % 4, 4))) for n in range(1, 8)]
    outer_group = [
        (n, ((lax.rem(cy + n // 4, 4) * 4 + lax.rem(cx + n % 4, 4)) * 2 + core, gy)) for n in range(1, 16)
    ]
    crossing = (lax.rem(gz + 31 + 2 * core, 32), gy)

    barrier = pltpu.get_barrier_semaphore()
    for _, peer in inner_group + outer_group + [(0, crossing)]:
        pl.semaphore_signal(barrier, inc=1, device_id=peer, device_id_type=MESH)
    pl.semaphore_wait(barrier, 23)

    def remote(src, dst, send, recv, peer):
        return pltpu.make_async_remote_copy(
            src_ref=src, dst_ref=dst, send_sem=send, recv_sem=recv, device_id=peer, device_id_type=MESH
        )

    sent = []

    def send(*args):
        copy = remote(*args)
        copy.start()
        sent.append(copy)

    def landed(dst, send_sem, recv_sem, peer):
        remote(dst, dst, send_sem, recv_sem, peer).wait_recv()

    body = pl.ds(8, 128)
    inner = pl.ds(1, 16)
    above, below = pl.ds(0, 8), pl.ds(136, 8)
    blocks = [pl.ds(cb * 128, 128) for cb in range(4)]
    for cb, cols in enumerate(blocks):
        send(vol.at[15, :, cols], pad.at[0, cb, body], hs.at[0, cb], hr.at[0, cb], g_next)
        send(vol.at[0, :, cols], pad.at[17, cb, body], hs.at[1, cb], hr.at[1, cb], g_prev)
    for cb, cols in enumerate(blocks):
        send(vol.at[:, pl.ds(120, 8), cols], pad.at[inner, cb, above], hs.at[2, cb], hr.at[2, cb], z_next)
        send(vol.at[:, pl.ds(0, 8), cols], pad.at[inner, cb, below], hs.at[3, cb], hr.at[3, cb], z_prev)

    groups = (4, 8, 12, 0)
    local = []
    parts = ((3, 6), (9, 4), (13, 3), (0, 3))
    for n, (first, many) in enumerate(parts):
        for cb, cols in enumerate(blocks):
            copy = pltpu.make_async_copy(
                vol.at[pl.ds(first, many), :, cols], pad.at[pl.ds(1 + first, many), cb, body], vsem.at[n, cb]
            )
            copy.start()
            local.append(copy)

    def volume_wait(n):
        for copy in local[n * 4 : n * 4 + 4]:
            copy.wait()

    def embed_copy(g):
        return pltpu.make_async_copy(
            emb.at[pl.ds(groups[g] * 256, 1024)], embuf.at[g % 2], lsem.at[4 + g % 2]
        )

    embed_copy(0).start()

    def own(t):
        return (up, down)[t % 2].at[t // 2]

    def rows(which, at, offset=0, size=NEAR):
        return pl.ds(which * FAR + at * NEAR + offset, size)

    def near(t, q, at):
        return wts.at[t // 2, t % 2, q, rows(core, at)]

    def half(t, q, at, h):
        return wts.at[t // 2, t % 2, q, rows(core, at, h * HALF, HALF)]

    seed_prev, seed_next, seed_far = lax.rem(seed + 3, 4), lax.rem(seed + 1, 4), lax.rem(seed + 2, 4)

    def step_z1(t):
        piece = own(t).at[rows(core, seed)]
        send(piece, near(t, gy, seed), z1s.at[t, 0], z1r.at[t, 0], z_next)
        send(piece, near(t, gy, seed), z1s.at[t, 1], z1r.at[t, 1], z_prev)

    def spread(t, n):
        piece = near(t, foreign[n], seed)
        send(piece, piece, a1s.at[t, n, 0], a1r.at[t, n, 0], a_next)
        send(piece, piece, a1s.at[t, n, 1], a1r.at[t, n, 1], a_prev)

    def step_b(t):
        landed(near(t, q_prev, seed), z1s.at[t, 0], z1r.at[t, 0], z_prev)
        piece = half(t, q_prev, seed, 0)
        send(piece, piece, z2s.at[t, 0], z2r.at[t, 0], z_next)
        spread(t, 0)
        landed(near(t, q_next, seed), z1s.at[t, 1], z1r.at[t, 1], z_next)
        piece = half(t, q_next, seed, 1)
        send(piece, piece, z2s.at[t, 1], z2r.at[t, 1], z_prev)
        spread(t, 1)

    def step_c(t):
        landed(half(t, q_far, seed, 0), z2s.at[t, 0], z2r.at[t, 0], z_prev)
        landed(half(t, q_far, seed, 1), z2s.at[t, 1], z2r.at[t, 1], z_next)
        spread(t, 2)

    def step_d(t, n):
        q = foreign[n]
        landed(near(t, q, seed_prev), a1s.at[t, n, 0], a1r.at[t, n, 0], a_prev)
        piece = half(t, q, seed_prev, 0)
        send(piece, piece, a2s.at[t, n, 0], a2r.at[t, n, 0], a_next)
        landed(near(t, q, seed_next), a1s.at[t, n, 1], a1r.at[t, n, 1], a_next)
        piece = half(t, q, seed_next, 1)
        send(piece, piece, a2s.at[t, n, 1], a2r.at[t, n, 1], a_prev)

    def step_e(t, n):
        q = foreign[n]
        landed(half(t, q, seed_far, 0), a2s.at[t, n, 0], a2r.at[t, n, 0], a_prev)
        landed(half(t, q, seed_far, 1), a2s.at[t, n, 1], a2r.at[t, n, 1], a_next)
        piece = wts.at[t // 2, t % 2, q, pl.ds(core * FAR, FAR)]
        send(piece, piece, ss.at[t, n], sr.at[t, n], twin)

    def step_f(t, n):
        dst = wts.at[t // 2, t % 2, foreign[n], pl.ds((1 - core) * FAR, FAR)]
        landed(dst, ss.at[t, n], sr.at[t, n], twin)

    order = [("z", 0), ("z", 1), ("b", 0), ("c", 0), ("z", 2), ("d", 0, 0), ("d", 0, 1), ("d", 0, 2)]
    order += [("b", 1), ("c", 1), ("e", 0, 0), ("e", 0, 1), ("e", 0, 2), ("z", 3)]
    order += [("d", 1, 0), ("d", 1, 1), ("d", 1, 2), ("b", 2), ("c", 2), ("f", 0, 0), ("f", 0, 1), ("f", 0, 2)]
    order += [("e", 1, 0), ("e", 1, 1), ("e", 1, 2), ("d", 2, 0), ("d", 2, 1), ("d", 2, 2), ("b", 3), ("c", 3)]
    order += [("f", 1, 0), ("f", 1, 1), ("f", 1, 2), ("e", 2, 0), ("e", 2, 1), ("e", 2, 2)]
    order += [("d", 3, 0), ("d", 3, 1), ("d", 3, 2), ("f", 2, 0), ("f", 2, 1), ("f", 2, 2)]
    order += [("e", 3, 0), ("e", 3, 1), ("e", 3, 2), ("f", 3, 0), ("f", 3, 1), ("f", 3, 2)]
    doing = {"z": step_z1, "b": step_b, "c": step_c, "d": step_d, "e": step_e, "f": step_f}

    def run_until(*last):
        while order:
            name, *args = order.pop(0)
            doing[name](*args)
            if (name, *args) == last:
                return

    run_until("z", 1)

    head_copy = pltpu.make_async_copy(head, headbuf, lsem.at[6])
    head_copy.start()
    gain_copy = pltpu.make_async_copy(gain, gainbuf, lsem.at[7])
    gain_copy.start()
    lab_copies = [
        pltpu.make_async_copy(lab.at[:, :, cols], labels.at[:, cb], labsem.at[cb]) for cb, cols in enumerate(blocks)
    ]
    mine = [
        pltpu.make_async_copy(own(t), wts.at[t // 2, t % 2, gy], lsem.at[9 + t]) for t in range(4)
    ]

    for cb in range(4):
        landed(pad.at[0, cb, body], hs.at[0, cb], hr.at[0, cb], g_prev)
        landed(pad.at[17, cb, body], hs.at[1, cb], hr.at[1, cb], g_next)
    corner = []
    for n, plane in enumerate((0, 17)):
        corner.append(remote(pad.at[plane, :, pl.ds(128, 8)], pad.at[plane, :, above], cs.at[n, 0], cr.at[n, 0], z_next))
        corner.append(remote(pad.at[plane, :, pl.ds(8, 8)], pad.at[plane, :, below], cs.at[n, 1], cr.at[n, 1], z_prev))
    for copy in corner:
        copy.start()
    for cb in range(4):
        landed(pad.at[inner, cb, above], hs.at[2, cb], hr.at[2, cb], z_prev)
        landed(pad.at[inner, cb, below], hs.at[3, cb], hr.at[3, cb], z_next)

    @pl.when(gy == 0)
    def _():
        pad[inner, :, above] = jnp.zeros((16, 4, 8, 128), F32)

    @pl.when(gy == 3)
    def _():
        pad[inner, :, below] = jnp.zeros((16, 4, 8, 128), F32)

    xacc[...] = jnp.zeros_like(xacc)
    lane = lax.broadcasted_iota(jnp.int32, (8, 512), 1)
    not_first, not_last = lane != 0, lane != 511
    block = lax.broadcasted_iota(jnp.int32, (8, 128), 1) // 16
    low = {bit: (block // bit) % 2 == 0 for bit in (1, 2, 4)}

    tap = {at: jnp.full((8, 128), taps[at], F32) for at in itertools.product(range(3), repeat=3)}

    def stem_row(d, i):
        totals = [[None] * 4 for third in range(3)]
        for first in range(3):
            for second in range(3):
                for cb in range(4):
                    x = pad[d + first, cb, pl.ds(7 + i + second, 8, stride=16), :]
                    for third in range(3):
                        term = tap[first, second, third] * x
                        before = totals[third][cb]
                        totals[third][cb] = term if before is None else before + term
        total = [jnp.concatenate(many, axis=1) for many in totals]
        left = jnp.where(not_first, pltpu.roll(total[0], 1, 1), 0.0)
        right = jnp.where(not_last, pltpu.roll(total[2], 511, 1), 0.0)
        v = 0.5 * (total[1] + left + right)
        v = v + v * jnp.tanh(v)
        stem[d, i] = v.astype(BF16).astype(F32)

    def stem_plane(d, at):
        @pl.loop(0, 16)
        def _(i):
            stem_row(d, i)

        for upper in range(2):
            for cb in range(4):
                v = [stem[d, upper * 8 + i, :, pl.ds(cb * 128, 128)] for i in range(8)]
                for bit in (1, 2, 4):
                    for i in range(8):
                        if i & bit == 0:
                            a, b = v[i], v[i + bit]
                            v[i] = jnp.where(low[bit], a, pltpu.roll(b, bit * 16, 1))
                            v[i + bit] = jnp.where(low[bit], pltpu.roll(a, 128 - bit * 16, 1), b)
                for m in range(4):
                    pair = jnp.concatenate([v[2 * m], v[2 * m + 1]], axis=0).astype(BF16)
                    cols = pl.ds(pl.multiple_of(at * 256 + upper * 128, 128), 128)
                    lhs[pl.ds(cb * 64 + m * 16, 16), cols] = pair

    def front(g):
        base = groups[g]

        @pl.loop(0, 4)
        def _(n):
            stem_plane(base + n, n)

        embed_copy(g).wait()
        slot = g % 2

        xacc[...] += jnp.dot(lhs[...], embuf[slot], preferred_element_type=F32)

    volume_wait(0)
    embed_copy(1).start()
    mine[0].start()
    mine[1].start()
    front(0)
    run_until("c", 0)
    volume_wait(1)
    embed_copy(2).start()
    front(1)
    run_until("d", 0, 2)
    for copy in corner:
        copy.wait()
    volume_wait(2)
    volume_wait(3)

    @pl.when(gz == 0)
    def _():
        pad[0] = jnp.zeros((4, 144, 128), F32)

    @pl.when(gz == 31)
    def _():
        pad[17] = jnp.zeros((4, 144, 128), F32)

    for plane in (0, 17):
        @pl.when(gy == 0)
        def _():
            pad[plane, :, above] = jnp.zeros((4, 8, 128), F32)

        @pl.when(gy == 3)
        def _():
            pad[plane, :, below] = jnp.zeros((4, 8, 128), F32)

    embed_copy(3).start()
    mine[2].start()
    mine[3].start()
    for copy in lab_copies:
        copy.start()
    front(2)
    run_until("e", 0, 2)
    front(3)
    run_until("c", 2)
    gain_copy.wait()
    for t in range(4):
        mine[t].wait()

    at_row = lax.broadcasted_iota(jnp.int32, (256, 512), 0) // 8
    at_col = lax.broadcasted_iota(jnp.int32, (256, 512), 1)
    for e in range(4):
        hit = jnp.logical_and(at_col // 16 == at_row, (at_col // 4) % 4 == e)
        expand[pl.ds(e * 256, 256)] = hit.astype(F32).astype(BF16)

    def as_stored(x):
        return x.astype(BF16).astype(F32)

    @pl.loop(0, 8)
    def _(n):
        at = pl.ds(pl.multiple_of(n * 32, 32), 32)
        xacc[at] = as_stored(xacc[at])

    def mlp_up(layer, q):
        u = jnp.dot(xn[...], wts[layer, 0, q], preferred_element_type=F32)
        hid[q] = jax.nn.gelu(u, approximate=True).astype(BF16)

    def mlp_down(layer, q):
        xacc[...] += jnp.dot(hid[q], wts[layer, 1, q], preferred_element_type=F32)

    for layer in range(2):
        @pl.loop(0, 8)
        def _(n):
            at = pl.ds(pl.multiple_of(n * 32, 32), 32)
            x = xacc[at]
            centred = x - jnp.mean(x, -1, keepdims=True)
            spread_ = jnp.mean(centred * centred, -1, keepdims=True)
            xn[at] = (centred * lax.rsqrt(spread_ + EPS) * gainbuf[pl.ds(layer, 1)]).astype(BF16)

        mlp_up(layer, gy)
        for n in range(3):
            run_until("f", 2 * layer, n)
            mlp_up(layer, foreign[n])
        mlp_down(layer, gy)
        for n in range(3):
            run_until("f", 2 * layer + 1, n)
            mlp_down(layer, foreign[n])

        @pl.loop(0, 8)
        def _(n):
            at = pl.ds(pl.multiple_of(n * 32, 32), 32)
            xacc[at] = as_stored(xacc[at])

    head_copy.wait()
    token = lax.broadcasted_iota(jnp.int32, (256, 256), 0)
    patch = (token % 8) * 32 + token // 8
    listed = jnp.max((slots[0] == patch).astype(F32), axis=1, keepdims=True)
    q = jnp.dot(xacc[...].astype(BF16), headbuf[...], preferred_element_type=F32)
    q = (as_stored(q) * listed).T
    coarse[0] = q[:, :128]
    coarse[1] = q[:, 128:]
    token = lax.broadcasted_iota(jnp.int32, (8, 256), 1)
    own_row = (token % 8 == lax.broadcasted_iota(jnp.int32, (8, 256), 0)).astype(F32)

    for c in range(4):
        spread_q = []
        for e in range(4):
            at = pl.ds(c * 64 + e, 16, stride=4)
            part = jnp.concatenate([coarse[0, at, :], coarse[1, at, :]], axis=1)
            spread_q.append((part[:, None, :] * own_row[None]).reshape(128, 256).astype(BF16))
        u = jnp.zeros((128, 512), F32)
        for e in range(4):
            u = u + jnp.dot(spread_q[e], expand[pl.ds(e * 256, 256)], preferred_element_type=F32)
        upq[pl.ds(c * 128, 128)] = 0.5 * (u + bias[c])
    for copy in lab_copies:
        copy.wait()

    half_skip = [0.5 * skip[c] for c in range(4)]
    for cb in range(4):
        cols = pl.ds(cb * 128, 128)

        def block_step(ab, carry):
            carry = list(carry)
            a, b = lax.div(ab, 4), lax.rem(ab, 4)
            level = [upq[pl.ds(pl.multiple_of(c * 128 + ab * 8, 8), 8), cols] for c in range(4)]
            for dd in range(4):
                for ii in range(4):
                    d, i = a * 4 + dd, b * 4 + ii
                    s = stem[d, i, :, cols]
                    l = labels[d, cb, pl.ds(i, 8, stride=16), :]
                    for c in range(4):
                        t = jnp.tanh(level[c] + half_skip[c] * s)
                        carry[c] = carry[c] + t
                        match = l == c
                        carry[4 + c] = carry[4 + c] + jnp.where(match, t, 0.0)
                        carry[8 + c] = carry[8 + c] + jnp.where(match, 1.0, 0.0)
            return tuple(carry)

        final = lax.fori_loop(0, 16, block_step, (jnp.zeros((8, 128), F32),) * 12)
        for c in range(4):
            sums[pl.ds(c * 8, 8), cols] = 0.5 * (final[4 + c] + final[8 + c])
            sums[pl.ds(32 + c * 8, 8), cols] = 8 * 16 + 0.5 * final[c]
            sums[pl.ds(64 + c * 8, 8), cols] = final[8 + c]

    fold = lax.broadcasted_iota(jnp.int32, (512, 256), 0) // 16 == lax.broadcasted_iota(jnp.int32, (512, 256), 1) % 32
    folded = jnp.dot(sums[...], fold.astype(F32), preferred_element_type=F32, precision=lax.Precision.HIGHEST)
    here = lax.broadcasted_iota(jnp.int32, (8, 256), 1) // 32 == lax.broadcasted_iota(jnp.int32, (8, 256), 0)
    lines = [
        jnp.sum(jnp.where(here, folded[n * 8 : n * 8 + 8], 0.0), axis=0, keepdims=True) for n in range(12)
    ]
    inter, mass, count = (jnp.concatenate(lines[n * 4 : n * 4 + 4], axis=0) for n in range(3))
    out[0, 0] = (2.0 * inter + 1.0) / (mass + count + 1.0)

    def send_line(x):
        return jnp.broadcast_to(jnp.sum(x, axis=1, keepdims=True), (4, 128))

    inbox[0] = jnp.concatenate(
        [send_line(inter), send_line(mass), send_line(count), jnp.zeros((4, 128), F32)], axis=0
    )
    for n, peer in inner_group:
        send(inbox.at[0], inbox.at[n], ps.at[n], pr.at[n], peer)
    for n, peer in inner_group:
        landed(inbox.at[n], ps.at[n], pr.at[n], peer)
    total = inbox[0]
    for n in range(1, 8):
        total = total + inbox[n]
    outbox[0] = total
    for n, peer in outer_group:
        send(outbox.at[0], outbox.at[n], ps.at[7 + n], pr.at[7 + n], peer)
    for n, peer in outer_group:
        landed(outbox.at[n], ps.at[7 + n], pr.at[7 + n], peer)
    for n in range(1, 16):
        total = total + outbox[n]
    ratio = (2.0 * total[0:4] + 1.0) / (total[4:8] + total[8:12] + 1.0)
    for c in range(4):
        dice[c] = ratio[c, 0]

    for copy in sent:
        copy.wait_send()


def per_device(
    volume, labels, patch_list, stem_kernel, embed_weight, norm_gain, up_weight, down_weight, head_weight, skip_weight, class_bias
):
    hbm = pl.BlockSpec(memory_space=pl.ANY)
    smem = pl.BlockSpec(memory_space=pltpu.SMEM)
    vmem = pl.BlockSpec(memory_space=pltpu.VMEM)
    dma = pltpu.SemaphoreType.DMA
    return pl.pallas_call(
        kernel,
        out_shape=(jax.ShapeDtypeStruct((1, 1, 4, 256), F32), jax.ShapeDtypeStruct((4,), F32)),
        in_specs=[hbm, hbm, vmem, smem, hbm, hbm, hbm, hbm, hbm, smem, smem],
        out_specs=(vmem, smem),
        scratch_shapes=[
            pltpu.VMEM((18, 4, 144, 128), F32),
            pltpu.VMEM((2, 2, 4, 1024, 1024), BF16),
            pltpu.VMEM((2, 1024, 1024), BF16),
            pltpu.VMEM((16, 16, 8, 512), F32),
            pltpu.VMEM((16, 4, 128, 128), jnp.int32),
            pltpu.VMEM((256, 1024), BF16),
            pltpu.VMEM((256, 1024), F32),
            pltpu.VMEM((256, 1024), BF16),
            pltpu.VMEM((4, 256, 1024), BF16),
            pltpu.VMEM((2, 256, 128), F32),
            pltpu.VMEM((512, 512), F32),
            pltpu.VMEM((1024, 512), BF16),
            pltpu.VMEM((96, 512), F32),
            pltpu.VMEM((1024, 256), BF16),
            pltpu.VMEM((2, 1024), F32),
            pltpu.VMEM((8, 16, 128), F32),
            pltpu.VMEM((16, 16, 128), F32),
            dma((4, 4)), dma((4, 4)), dma((2, 2)), dma((2, 2)), dma((4, 4)), dma((4,)),
            dma((4, 2)), dma((4, 2)), dma((4, 2)), dma((4, 2)),
            dma((4, 3, 2)), dma((4, 3, 2)), dma((4, 3, 2)), dma((4, 3, 2)),
            dma((4, 3)), dma((4, 3)),
            dma((23,)), dma((23,)),
            dma((13,)),
        ],
        compiler_params=pltpu.CompilerParams(
            collective_id=0, has_side_effects=True, vmem_limit_bytes=60 * 1024 * 1024
        ),
    )(
        volume, labels, patch_list, stem_kernel, embed_weight, norm_gain,
        up_weight, down_weight, head_weight, skip_weight, class_bias,
    )


def solution(mesh):
    placed = (
        P("gz", "gy", None),
        P("gz", "gy", None),
        P("gz", "gy", None),
        P(),
        P(),
        P(),
        P(None, None, "gy"),
        P(None, "gy", None),
        P(),
        P(),
        P(),
    )
    return jax.shard_map(
        per_device,
        mesh=mesh,
        in_specs=placed,
        out_specs=(P("gz", "gy", None, None), P()),
        check_vma=False,
    )
```

```python
import itertools

import jax
import jax.numpy as jnp
from jax import lax
from jax.experimental import pallas as pl
from jax.experimental.pallas import tpu as pltpu
from jax.sharding import PartitionSpec as P

EPS = 1e-05
MESH = pl.DeviceIdType.MESH
F32 = jnp.float32
BF16 = jnp.bfloat16

SIDE, PIECE, STRAIGHT = 512, 112, 64
STAGES = ((0, 0, 0, 1024), (0, 1, 0, 1024), (1, 0, 0, 1024), (1, 1, 0, 1024))


def kernel(
    vol, lab, slots, taps, emb, gain, up, down, head, skip, bias,
    out, dice,
    pad, wts, embuf, stem, labels, lhs, xacc, xn, hid, coarse, upq, expand, sums, headbuf, gainbuf, edge, inbox, outbox,
    hs, hr, cs, cr, vsem, labsem, z1s, z1r, z2s, z2r, s1s, s1r, s2s, s2r, a1s, a1r, a2s, a2r, tws, twr, ps, pr, lsem,
):
    gz, gy = lax.axis_index("gz"), lax.axis_index("gy")
    core = lax.rem(gz, 2)
    chip = lax.div(gz, 2)
    cx, cy = lax.rem(chip, 4), lax.div(chip, 4)
    seed = (1 - core) * cx + core * cy

    def along(step):
        first = (cy * 4 + lax.rem(cx + step, 4)) * 2
        second = (lax.rem(cy + step, 4) * 4 + cx) * 2 + 1
        return ((1 - core) * first + core * second, gy)

    z_next, z_prev = (gz, lax.rem(gy + 1, 4)), (gz, lax.rem(gy + 3, 4))
    a_next, a_prev = along(1), along(3)
    g_next, g_prev = (lax.rem(gz + 1, 32), gy), (lax.rem(gz + 31, 32), gy)
    twin = (gz + 1 - 2 * core, gy)
    q_prev, q_next, q_far = lax.rem(gy + 3, 4), lax.rem(gy + 1, 4), lax.rem(gy + 2, 4)
    foreign = (q_prev, q_next, q_far)

    inner_group = [(n, (chip * 2 + lax.rem(core + n // 4, 2), lax.rem(gy + n % 4, 4))) for n in range(1, 8)]
    outer_group = [
        (n, ((lax.rem(cy + n // 4, 4) * 4 + lax.rem(cx + n % 4, 4)) * 2 + core, gy)) for n in range(1, 16)
    ]
    crossing = (lax.rem(gz + 31 + 2 * core, 32), gy)

    barrier = pltpu.get_barrier_semaphore()
    for _, peer in inner_group + outer_group + [(0, crossing)]:
        pl.semaphore_signal(barrier, inc=1, device_id=peer, device_id_type=MESH)
    pl.semaphore_wait(barrier, 23)

    def remote(src, dst, send, recv, peer):
        return pltpu.make_async_remote_copy(
            src_ref=src, dst_ref=dst, send_sem=send, recv_sem=recv, device_id=peer, device_id_type=MESH
        )

    z1, z2, s1, s2, a1, a2, tw = (z1s, z1r), (z2s, z2r), (s1s, s1r), (s2s, s2r), (a1s, a1r), (a2s, a2r), (tws, twr)
    sent = []

    def send(*args):
        copy = remote(*args)
        copy.start()
        sent.append(copy)

    def landed(dst, send_sem, recv_sem, peer):
        remote(dst, dst, send_sem, recv_sem, peer).wait_recv()

    body = pl.ds(8, 128)
    inner = pl.ds(1, 16)
    above, below = pl.ds(0, 8), pl.ds(136, 8)
    blocks = [pl.ds(cb * 128, 128) for cb in range(4)]
    for cb, cols in enumerate(blocks):
        send(vol.at[:, 127, cols], edge.at[0, cb], hs.at[2, cb], hr.at[2, cb], z_next)
        send(vol.at[:, 0, cols], edge.at[1, cb], hs.at[3, cb], hr.at[3, cb], z_prev)
    for cb, cols in enumerate(blocks):
        send(vol.at[15, :, cols], pad.at[0, cb, body], hs.at[0, cb], hr.at[0, cb], g_next)
        send(vol.at[0, :, cols], pad.at[17, cb, body], hs.at[1, cb], hr.at[1, cb], g_prev)

    groups = (4, 8, 12, 0)
    local = []
    parts = ((3, 6), (9, 4), (13, 3), (0, 3))
    for n, (first, many) in enumerate(parts):
        for cb, cols in enumerate(blocks):
            copy = pltpu.make_async_copy(
                vol.at[pl.ds(first, many), :, cols], pad.at[pl.ds(1 + first, many), cb, body], vsem.at[n, cb]
            )
            copy.start()
            local.append(copy)

    def volume_wait(n):
        for copy in local[n * 4 : n * 4 + 4]:
            copy.wait()

    def embed_copy(g):
        return pltpu.make_async_copy(
            emb.at[pl.ds(groups[g] * 256, 1024)], embuf.at[g % 2], lsem.at[4 + g % 2]
        )

    embed_copy(0).start()

    def view(t, q, at):
        layer, matrix, first, width = STAGES[t]
        return wts.at[layer, matrix, q, at, pl.ds(first, width)]

    def own(t, at):
        layer, matrix, first, width = STAGES[t]
        return (up, down)[matrix].at[layer, at, pl.ds(first, width)]

    seed_prev, seed_next, seed_far = lax.rem(seed + 3, 4), lax.rem(seed + 1, 4), lax.rem(seed + 2, 4)

    def piece(at):
        return pl.ds(core * SIDE + at * PIECE, PIECE)

    def part(at, h, odd):
        first = 48 if odd else 64
        return pl.ds(core * SIDE + at * PIECE + h * first, PIECE - first if h else first)

    def straight(h=None):
        if h is None:
            return pl.ds(core * SIDE + 4 * PIECE, STRAIGHT)
        return pl.ds(core * SIDE + 4 * PIECE + h * (STRAIGHT // 2), STRAIGHT // 2)

    def pass_on(t, q, at, sems, index, peer):
        send(view(t, q, at), view(t, q, at), sems[0].at[index], sems[1].at[index], peer)

    def await_(t, q, at, sems, index, peer):
        landed(view(t, q, at), sems[0].at[index], sems[1].at[index], peer)

    def first_z(t, at, sems):
        send(own(t, at), view(t, gy, at), sems[0].at[t, 0], sems[1].at[t, 0], z_next)
        send(own(t, at), view(t, gy, at), sems[0].at[t, 1], sems[1].at[t, 1], z_prev)

    def spread(t, n):
        pass_on(t, foreign[n], piece(seed), a1, (t, n, 0), a_next)
        pass_on(t, foreign[n], piece(seed), a1, (t, n, 1), a_prev)

    def step_z(t):
        first_z(t, piece(seed), z1)

    def step_b(t, n):
        peer, other = ((z_prev, z_next), (z_next, z_prev))[n]
        await_(t, foreign[n], piece(seed), z1, (t, n), peer)
        pass_on(t, foreign[n], part(seed, n, t % 2), z2, (t, n), other)
        spread(t, n)

    def step_c(t):
        await_(t, q_far, part(seed, 0, t % 2), z2, (t, 0), z_prev)
        await_(t, q_far, part(seed, 1, t % 2), z2, (t, 1), z_next)
        spread(t, 2)

    def step_s(t):
        first_z(t, straight(), s1)

    def step_t(t):
        await_(t, q_prev, straight(), s1, (t, 0), z_prev)
        pass_on(t, q_prev, straight(0), s2, (t, 0), z_next)
        await_(t, q_next, straight(), s1, (t, 1), z_next)
        pass_on(t, q_next, straight(1), s2, (t, 1), z_prev)

    def step_u(t):
        await_(t, q_far, straight(0), s2, (t, 0), z_prev)
        await_(t, q_far, straight(1), s2, (t, 1), z_next)

    def step_d(t, n):
        q, odd = foreign[n], (t + n) % 2
        await_(t, q, piece(seed_prev), a1, (t, n, 0), a_prev)
        pass_on(t, q, part(seed_prev, 0, odd), a2, (t, n, 0), a_next)
        await_(t, q, piece(seed_next), a1, (t, n, 1), a_next)
        pass_on(t, q, part(seed_next, 1, odd), a2, (t, n, 1), a_prev)

    def step_e(t, n):
        q, odd = foreign[n], (t + n) % 2
        await_(t, q, part(seed_far, 0, odd), a2, (t, n, 0), a_prev)
        await_(t, q, part(seed_far, 1, odd), a2, (t, n, 1), a_next)
        pass_on(t, q, pl.ds(core * SIDE, SIDE), tw, (t, n), twin)

    def step_f(t, n):
        await_(t, foreign[n], pl.ds((1 - core) * SIDE, SIDE), tw, (t, n), twin)

    doing = {
        "z": step_z, "b": step_b, "c": step_c, "s": step_s, "t": step_t, "u": step_u, "d": step_d, "e": step_e, "f": step_f,
    }
    plan = [
        (0.0, 'z', 0), (0.0, 'z', 1), (0.0, 's', 0), (6.3, 'b', 0, 0), (6.3, 'b', 0, 1),
        (6.3, 'z', 2), (6.3, 's', 1), (10.0, 'd', 0, 0), (11.4, 'b', 1, 0), (11.4, 'b', 1, 1),
        (11.4, 'z', 3), (11.4, 's', 2), (12.6, 'd', 0, 1), (14.3, 't', 0), (14.3, 'e', 0, 0),
        (16.4, 'd', 1, 0), (16.9, 'c', 0), (17.3, 'f', 0, 0), (19.0, 'd', 1, 1), (20.2, 'e', 0, 1),
        (22.0, 'b', 2, 0), (22.0, 'b', 2, 1), (23.2, 'f', 0, 1), (24.1, 'd', 0, 2), (24.9, 't', 1),
        (24.9, 'e', 1, 0), (25.3, 'e', 1, 1), (27.4, 'c', 1), (27.8, 'f', 1, 0), (27.9, 'd', 2, 0),
        (29.6, 'f', 1, 1), (30.4, 'd', 2, 1), (32.5, 'b', 3, 0), (32.5, 'b', 3, 1), (32.5, 's', 3),
        (34.3, 'd', 1, 2), (35.4, 't', 2), (35.5, 'e', 2, 0), (36.8, 'e', 2, 1), (36.9, 'u', 0),
        (36.9, 'e', 0, 2), (38.5, 'f', 2, 0), (39.4, 'd', 3, 0), (39.4, 'c', 2), (40.2, 'f', 2, 1),
        (40.9, 'u', 1), (41.9, 'd', 3, 1), (42.0, 'f', 0, 2), (43.2, 'e', 1, 2), (43.4, 'c', 3),
        (46.1, 'f', 1, 2), (46.3, 't', 3), (46.3, 'e', 3, 0), (47.0, 'd', 2, 2), (47.8, 'u', 2),
        (48.3, 'e', 3, 1), (49.3, 'u', 3), (49.3, 'f', 3, 0), (50.8, 'd', 3, 2), (51.2, 'f', 3, 1),
        (52.1, 'e', 2, 2), (53.4, 'e', 3, 2), (55.0, 'f', 2, 2), (56.8, 'f', 3, 2),
    ]

    done = set()

    def run_until(when=None, last=None):
        while plan and last not in done:
            if when is not None and plan[0][0] > when:
                return
            _, *step = plan.pop(0)
            doing[step[0]](*step[1:])
            done.add(tuple(step))

    run_until(0.0)

    head_copy = pltpu.make_async_copy(head, headbuf, lsem.at[6])
    head_copy.start()
    gain_copy = pltpu.make_async_copy(gain, gainbuf, lsem.at[7])
    gain_copy.start()
    lab_copies = [
        pltpu.make_async_copy(lab.at[:, :, cols], labels.at[:, cb], labsem.at[cb]) for cb, cols in enumerate(blocks)
    ]
    mine = [
        pltpu.make_async_copy((up, down)[t % 2].at[t // 2], wts.at[t // 2, t % 2, gy], lsem.at[9 + t]) for t in range(4)
    ]

    for cb in range(4):
        landed(pad.at[0, cb, body], hs.at[0, cb], hr.at[0, cb], g_prev)
        landed(pad.at[17, cb, body], hs.at[1, cb], hr.at[1, cb], g_next)
    corner = []
    for n, plane in enumerate((0, 17)):
        corner.append(remote(pad.at[plane, :, pl.ds(128, 8)], pad.at[plane, :, above], cs.at[n, 0], cr.at[n, 0], z_next))
        corner.append(remote(pad.at[plane, :, pl.ds(8, 8)], pad.at[plane, :, below], cs.at[n, 1], cr.at[n, 1], z_prev))
    for copy in corner:
        copy.start()
    for cb in range(4):
        landed(edge.at[0, cb], hs.at[2, cb], hr.at[2, cb], z_prev)
        landed(edge.at[1, cb], hs.at[3, cb], hr.at[3, cb], z_next)
    keep_above, keep_below = (gy > 0).astype(F32), (gy < 3).astype(F32)
    for cb in range(4):
        for d in range(16):
            pad[1 + d, cb, pl.ds(7, 1)] = edge[0, cb, pl.ds(d, 1)] * keep_above
            pad[1 + d, cb, pl.ds(136, 1)] = edge[1, cb, pl.ds(d, 1)] * keep_below

    xacc[...] = jnp.zeros_like(xacc)
    lane = lax.broadcasted_iota(jnp.int32, (8, 512), 1)
    not_first, not_last = lane != 0, lane != 511
    block = lax.broadcasted_iota(jnp.int32, (8, 128), 1) // 16
    low = {bit: (block // bit) % 2 == 0 for bit in (1, 2, 4)}

    tap = {at: jnp.full((8, 128), taps[at], F32) for at in itertools.product(range(3), repeat=3)}

    def stem_rows(d, first_row, many=8):
        totals = [[[None] * 4 for third in range(3)] for _ in range(many)]
        for first in range(3):
            for row in range(many + 2):
                for cb in range(4):
                    x = pad[d + first, cb, pl.ds(7 + first_row + row, 8, stride=16), :]
                    for second in range(3):
                        if 0 <= row - second < many:
                            mine_ = totals[row - second]
                            for third in range(3):
                                term = tap[first, second, third] * x
                                mine_[third][cb] = term if mine_[third][cb] is None else mine_[third][cb] + term
        for n in range(many):
            total = [jnp.concatenate(blocks_, axis=1) for blocks_ in totals[n]]
            left = jnp.where(not_first, pltpu.roll(total[0], 1, 1), 0.0)
            right = jnp.where(not_last, pltpu.roll(total[2], 511, 1), 0.0)
            v = 0.5 * (total[1] + left + right)
            v = v + v * jnp.tanh(v)
            stem[d, first_row + n] = v.astype(BF16).astype(F32)

    def stem_plane(d, at):
        @pl.loop(0, 2)
        def _(n):
            stem_rows(d, n * 8)

        for upper in range(2):
            for cb in range(4):
                v = [stem[d, upper * 8 + i, :, pl.ds(cb * 128, 128)] for i in range(8)]
                for bit in (1, 2, 4):
                    for i in range(8):
                        if i & bit == 0:
                            a, b = v[i], v[i + bit]
                            v[i] = jnp.where(low[bit], a, pltpu.roll(b, bit * 16, 1))
                            v[i + bit] = jnp.where(low[bit], pltpu.roll(a, 128 - bit * 16, 1), b)
                for m in range(4):
                    pair = jnp.concatenate([v[2 * m], v[2 * m + 1]], axis=0).astype(BF16)
                    cols = pl.ds(pl.multiple_of(at * 256 + upper * 128, 128), 128)
                    lhs[pl.ds(cb * 64 + m * 16, 16), cols] = pair

    def front(g, last):
        base = groups[g]

        for first in (0, 2):
            @pl.loop(first, first + 2)
            def _(n):
                stem_plane(base + n, n)

            if first == 0:
                run_until(last - 2.3)

        embed_copy(g).wait()
        xacc[...] += jnp.dot(lhs[...], embuf[g % 2], preferred_element_type=F32)
        run_until(last)

    volume_wait(0)
    embed_copy(1).start()
    mine[0].start()
    mine[1].start()
    front(0, 8)
    volume_wait(1)
    embed_copy(2).start()
    front(1, 12)
    for copy in corner:
        copy.wait()
    volume_wait(2)
    volume_wait(3)

    @pl.when(gz == 0)
    def _():
        pad[0] = jnp.zeros((4, 144, 128), F32)

    @pl.when(gz == 31)
    def _():
        pad[17] = jnp.zeros((4, 144, 128), F32)

    for plane in (0, 17):
        @pl.when(gy == 0)
        def _():
            pad[plane, :, above] = jnp.zeros((4, 8, 128), F32)

        @pl.when(gy == 3)
        def _():
            pad[plane, :, below] = jnp.zeros((4, 8, 128), F32)

    embed_copy(3).start()
    mine[2].start()
    mine[3].start()
    for copy in lab_copies:
        copy.start()
    front(2, 16)
    front(3, 20)
    gain_copy.wait()
    for t in range(4):
        mine[t].wait()

    at_row = lax.broadcasted_iota(jnp.int32, (256, 512), 0) // 8
    at_col = lax.broadcasted_iota(jnp.int32, (256, 512), 1)
    for e in range(4):
        hit = jnp.logical_and(at_col // 16 == at_row, (at_col // 4) % 4 == e)
        expand[pl.ds(e * 256, 256)] = hit.astype(F32).astype(BF16)

    def as_stored(x):
        return x.astype(BF16).astype(F32)

    @pl.loop(0, 8)
    def _(n):
        at = pl.ds(pl.multiple_of(n * 32, 32), 32)
        xacc[at] = as_stored(xacc[at])

    def mlp_up(layer, q):
        u = jnp.dot(xn[...], wts[layer, 0, q], preferred_element_type=F32)
        hid[q] = jax.nn.gelu(u, approximate=True).astype(BF16)

    def mlp_down(layer, q):
        xacc[...] += jnp.dot(hid[q], wts[layer, 1, q], preferred_element_type=F32)

    for layer in range(2):
        @pl.loop(0, 8)
        def _(n):
            at = pl.ds(pl.multiple_of(n * 32, 32), 32)
            x = xacc[at]
            centred = x - jnp.mean(x, -1, keepdims=True)
            spread_ = jnp.mean(centred * centred, -1, keepdims=True)
            xn[at] = (centred * lax.rsqrt(spread_ + EPS) * gainbuf[pl.ds(layer, 1)]).astype(BF16)

        mlp_up(layer, gy)
        for n in range(3):
            run_until(last=("f", 0 if layer == 0 else 2, n))
            mlp_up(layer, foreign[n])
        mlp_down(layer, gy)
        for n in range(3):
            run_until(last=("f", 1 if layer == 0 else 3, n))
            mlp_down(layer, foreign[n])

        @pl.loop(0, 8)
        def _(n):
            at = pl.ds(pl.multiple_of(n * 32, 32), 32)
            xacc[at] = as_stored(xacc[at])

    head_copy.wait()
    token = lax.broadcasted_iota(jnp.int32, (256, 256), 0)
    patch = (token % 8) * 32 + token // 8
    listed = jnp.max((slots[0] == patch).astype(F32), axis=1, keepdims=True)
    q = jnp.dot(xacc[...].astype(BF16), headbuf[...], preferred_element_type=F32)
    q = (as_stored(q) * listed).T
    coarse[0] = q[:, :128]
    coarse[1] = q[:, 128:]
    token = lax.broadcasted_iota(jnp.int32, (8, 256), 1)
    own_row = (token % 8 == lax.broadcasted_iota(jnp.int32, (8, 256), 0)).astype(F32)

    for c in range(4):
        spread_q = []
        for e in range(4):
            at = pl.ds(c * 64 + e, 16, stride=4)
            part = jnp.concatenate([coarse[0, at, :], coarse[1, at, :]], axis=1)
            spread_q.append((part[:, None, :] * own_row[None]).reshape(128, 256).astype(BF16))
        u = jnp.zeros((128, 512), F32)
        for e in range(4):
            u = u + jnp.dot(spread_q[e], expand[pl.ds(e * 256, 256)], preferred_element_type=F32)
        upq[pl.ds(c * 128, 128)] = 0.5 * (u + bias[c])
    for copy in lab_copies:
        copy.wait()

    half_skip = [0.5 * skip[c] for c in range(4)]
    for cb in range(4):
        cols = pl.ds(cb * 128, 128)

        def block_step(ab, carry):
            carry = list(carry)
            a, b = lax.div(ab, 4), lax.rem(ab, 4)
            level = [upq[pl.ds(pl.multiple_of(c * 128 + ab * 8, 8), 8), cols] for c in range(4)]
            for dd in range(4):
                for ii in range(4):
                    d, i = a * 4 + dd, b * 4 + ii
                    s = stem[d, i, :, cols]
                    l = labels[d, cb, pl.ds(i, 8, stride=16), :]
                    for c in range(4):
                        t = jnp.tanh(level[c] + half_skip[c] * s)
                        carry[c] = carry[c] + t
                        match = l == c
                        carry[4 + c] = carry[4 + c] + jnp.where(match, t, 0.0)
                        carry[8 + c] = carry[8 + c] + jnp.where(match, 1.0, 0.0)
            return tuple(carry)

        final = lax.fori_loop(0, 16, block_step, (jnp.zeros((8, 128), F32),) * 12)
        for c in range(4):
            sums[pl.ds(c * 8, 8), cols] = 0.5 * (final[4 + c] + final[8 + c])
            sums[pl.ds(32 + c * 8, 8), cols] = 8 * 16 + 0.5 * final[c]
            sums[pl.ds(64 + c * 8, 8), cols] = final[8 + c]

    fold = lax.broadcasted_iota(jnp.int32, (512, 256), 0) // 16 == lax.broadcasted_iota(jnp.int32, (512, 256), 1) % 32
    folded = jnp.dot(sums[...], fold.astype(F32), preferred_element_type=F32, precision=lax.Precision.HIGHEST)
    here = lax.broadcasted_iota(jnp.int32, (8, 256), 1) // 32 == lax.broadcasted_iota(jnp.int32, (8, 256), 0)
    lines = [
        jnp.sum(jnp.where(here, folded[n * 8 : n * 8 + 8], 0.0), axis=0, keepdims=True) for n in range(12)
    ]
    inter, mass, count = (jnp.concatenate(lines[n * 4 : n * 4 + 4], axis=0) for n in range(3))
    out[0, 0] = (2.0 * inter + 1.0) / (mass + count + 1.0)

    def send_line(x):
        return jnp.broadcast_to(jnp.sum(x, axis=1, keepdims=True), (4, 128))

    inbox[0] = jnp.concatenate(
        [send_line(inter), send_line(mass), send_line(count), jnp.zeros((4, 128), F32)], axis=0
    )
    for n, peer in inner_group:
        send(inbox.at[0], inbox.at[n], ps.at[n], pr.at[n], peer)
    for n, peer in inner_group:
        landed(inbox.at[n], ps.at[n], pr.at[n], peer)
    total = inbox[0]
    for n in range(1, 8):
        total = total + inbox[n]
    outbox[0] = total
    for n, peer in outer_group:
        send(outbox.at[0], outbox.at[n], ps.at[7 + n], pr.at[7 + n], peer)
    for n, peer in outer_group:
        landed(outbox.at[n], ps.at[7 + n], pr.at[7 + n], peer)
    for n in range(1, 16):
        total = total + outbox[n]
    ratio = (2.0 * total[0:4] + 1.0) / (total[4:8] + total[8:12] + 1.0)
    for c in range(4):
        dice[c] = ratio[c, 0]

    assert not plan
    for copy in sent:
        copy.wait_send()


def per_device(
    volume, labels, patch_list, stem_kernel, embed_weight, norm_gain, up_weight, down_weight, head_weight, skip_weight, class_bias
):
    hbm = pl.BlockSpec(memory_space=pl.ANY)
    smem = pl.BlockSpec(memory_space=pltpu.SMEM)
    vmem = pl.BlockSpec(memory_space=pltpu.VMEM)
    dma = pltpu.SemaphoreType.DMA
    return pl.pallas_call(
        kernel,
        out_shape=(jax.ShapeDtypeStruct((1, 1, 4, 256), F32), jax.ShapeDtypeStruct((4,), F32)),
        in_specs=[hbm, hbm, vmem, smem, hbm, hbm, hbm, hbm, hbm, smem, smem],
        out_specs=(vmem, smem),
        scratch_shapes=[
            pltpu.VMEM((18, 4, 144, 128), F32),
            pltpu.VMEM((2, 2, 4, 1024, 1024), BF16),
            pltpu.VMEM((2, 1024, 1024), BF16),
            pltpu.VMEM((16, 16, 8, 512), F32),
            pltpu.VMEM((16, 4, 128, 128), jnp.int32),
            pltpu.VMEM((256, 1024), BF16),
            pltpu.VMEM((256, 1024), F32),
            pltpu.VMEM((256, 1024), BF16),
            pltpu.VMEM((4, 256, 1024), BF16),
            pltpu.VMEM((2, 256, 128), F32),
            pltpu.VMEM((512, 512), F32),
            pltpu.VMEM((1024, 512), BF16),
            pltpu.VMEM((96, 512), F32),
            pltpu.VMEM((1024, 256), BF16),
            pltpu.VMEM((2, 1024), F32),
            pltpu.VMEM((2, 4, 16, 128), F32),
            pltpu.VMEM((8, 16, 128), F32),
            pltpu.VMEM((16, 16, 128), F32),
            dma((4, 4)), dma((4, 4)), dma((2, 2)), dma((2, 2)), dma((4, 4)), dma((4,)),
            dma((4, 2)), dma((4, 2)), dma((4, 2)), dma((4, 2)),
            dma((4, 2)), dma((4, 2)), dma((4, 2)), dma((4, 2)),
            dma((4, 3, 2)), dma((4, 3, 2)), dma((4, 3, 2)), dma((4, 3, 2)),
            dma((4, 3)), dma((4, 3)),
            dma((23,)), dma((23,)),
            dma((13,)),
        ],
        compiler_params=pltpu.CompilerParams(
            collective_id=0, has_side_effects=True, vmem_limit_bytes=60 * 1024 * 1024
        ),
    )(
        volume, labels, patch_list, stem_kernel, embed_weight, norm_gain,
        up_weight, down_weight, head_weight, skip_weight, class_bias,
    )


def solution(mesh):
    placed = (
        P("gz", "gy", None),
        P("gz", "gy", None),
        P("gz", "gy", None),
        P(),
        P(),
        P(),
        P(None, None, "gy"),
        P(None, "gy", None),
        P(),
        P(),
        P(),
    )
    return jax.shard_map(
        per_device,
        mesh=mesh,
        in_specs=placed,
        out_specs=(P("gz", "gy", None, None), P()),
        check_vma=False,
    )
```

```python
import itertools

import jax
import jax.numpy as jnp
from jax import lax
from jax.experimental import pallas as pl
from jax.experimental.pallas import tpu as pltpu
from jax.sharding import PartitionSpec as P

EPS = 1e-05
MESH = pl.DeviceIdType.MESH
F32 = jnp.float32
BF16 = jnp.bfloat16

SIDE, PIECE, STRAIGHT = 512, 112, 64
STAGES = ((0, 0, 0, 512), (0, 0, 512, 512), (0, 1, 0, 512), (0, 1, 512, 512), (1, 0, 0, 512), (1, 0, 512, 512), (1, 1, 0, 512), (1, 1, 512, 512))


def kernel(
    vol, lab, slots, taps, emb, gain, up, down, head, skip, bias,
    out, dice,
    pad, wts, embuf, stem, labels, lhs, xacc, xn, hid, coarse, upq, expand, sums, headbuf, gainbuf, edge, inbox, outbox,
    hs, hr, cs, cr, vsem, labsem, z1s, z1r, z2s, z2r, s1s, s1r, s2s, s2r, a1s, a1r, a2s, a2r, tws, twr, ps, pr, lsem,
):
    gz, gy = lax.axis_index("gz"), lax.axis_index("gy")
    core = lax.rem(gz, 2)
    chip = lax.div(gz, 2)
    cx, cy = lax.rem(chip, 4), lax.div(chip, 4)
    seed = (1 - core) * cx + core * cy

    def along(step):
        first = (cy * 4 + lax.rem(cx + step, 4)) * 2
        second = (lax.rem(cy + step, 4) * 4 + cx) * 2 + 1
        return ((1 - core) * first + core * second, gy)

    z_next, z_prev = (gz, lax.rem(gy + 1, 4)), (gz, lax.rem(gy + 3, 4))
    a_next, a_prev = along(1), along(3)
    g_next, g_prev = (lax.rem(gz + 1, 32), gy), (lax.rem(gz + 31, 32), gy)
    twin = (gz + 1 - 2 * core, gy)
    q_prev, q_next, q_far = lax.rem(gy + 3, 4), lax.rem(gy + 1, 4), lax.rem(gy + 2, 4)
    foreign = (q_prev, q_next, q_far)

    inner_group = [(n, (chip * 2 + lax.rem(core + n // 4, 2), lax.rem(gy + n % 4, 4))) for n in range(1, 8)]
    outer_group = [
        (n, ((lax.rem(cy + n // 4, 4) * 4 + lax.rem(cx + n % 4, 4)) * 2 + core, gy)) for n in range(1, 16)
    ]
    crossing = (lax.rem(gz + 31 + 2 * core, 32), gy)

    body, inner = pl.ds(8, 128), pl.ds(1, 16)
    above, below = pl.ds(0, 8), pl.ds(136, 8)
    blocks = [pl.ds(cb * 128, 128) for cb in range(4)]
    groups = (4, 8, 12, 0)
    local = []
    parts = ((3, 6), (9, 4), (13, 3), (0, 3))
    for n, (first, many) in enumerate(parts):
        for cb, cols in enumerate(blocks):
            copy = pltpu.make_async_copy(
                vol.at[pl.ds(first, many), :, cols], pad.at[pl.ds(1 + first, many), cb, body], vsem.at[n, cb]
            )
            copy.start()
            local.append(copy)

    def volume_wait(n):
        for copy in local[n * 4 : n * 4 + 4]:
            copy.wait()

    def embed_copy(g):
        return pltpu.make_async_copy(
            emb.at[pl.ds(groups[g] * 256, 1024)], embuf.at[g % 2], lsem.at[4 + g % 2]
        )

    embed_copy(0).start()
    embed_copy(1).start()

    barrier = pltpu.get_barrier_semaphore()
    for _, peer in inner_group + outer_group + [(0, crossing)]:
        pl.semaphore_signal(barrier, inc=1, device_id=peer, device_id_type=MESH)
    pl.semaphore_wait(barrier, 23)

    def remote(src, dst, send, recv, peer):
        return pltpu.make_async_remote_copy(
            src_ref=src, dst_ref=dst, send_sem=send, recv_sem=recv, device_id=peer, device_id_type=MESH
        )

    z1, z2, s1, s2, a1, a2, tw = (z1s, z1r), (z2s, z2r), (s1s, s1r), (s2s, s2r), (a1s, a1r), (a2s, a2r), (tws, twr)
    sent = []

    def send(*args):
        copy = remote(*args)
        copy.start()
        sent.append(copy)

    def landed(dst, send_sem, recv_sem, peer):
        remote(dst, dst, send_sem, recv_sem, peer).wait_recv()

    for cb, cols in enumerate(blocks):
        send(vol.at[:, 127, cols], edge.at[0, cb], hs.at[2, cb], hr.at[2, cb], z_next)
        send(vol.at[:, 0, cols], edge.at[1, cb], hs.at[3, cb], hr.at[3, cb], z_prev)
    for cb, cols in enumerate(blocks):
        send(vol.at[15, :, cols], pad.at[0, cb, body], hs.at[0, cb], hr.at[0, cb], g_next)
        send(vol.at[0, :, cols], pad.at[17, cb, body], hs.at[1, cb], hr.at[1, cb], g_prev)

    def view(t, q, at):
        layer, matrix, first, width = STAGES[t]
        return wts.at[layer, matrix, q, at, pl.ds(first, width)]

    def own(t, at):
        layer, matrix, first, width = STAGES[t]
        return (up, down)[matrix].at[layer, at, pl.ds(first, width)]

    seed_prev, seed_next, seed_far = lax.rem(seed + 3, 4), lax.rem(seed + 1, 4), lax.rem(seed + 2, 4)

    def piece(at):
        return pl.ds(core * SIDE + at * PIECE, PIECE)

    def part(at, h, odd):
        first = 48 if odd else 64
        return pl.ds(core * SIDE + at * PIECE + h * first, PIECE - first if h else first)

    def straight(h=None):
        if h is None:
            return pl.ds(core * SIDE + 4 * PIECE, STRAIGHT)
        return pl.ds(core * SIDE + 4 * PIECE + h * (STRAIGHT // 2), STRAIGHT // 2)

    def pass_on(t, q, at, sems, index, peer):
        send(view(t, q, at), view(t, q, at), sems[0].at[index], sems[1].at[index], peer)

    def await_(t, q, at, sems, index, peer):
        landed(view(t, q, at), sems[0].at[index], sems[1].at[index], peer)

    def first_z(t, at, sems):
        send(own(t, at), view(t, gy, at), sems[0].at[t, 0], sems[1].at[t, 0], z_next)
        send(own(t, at), view(t, gy, at), sems[0].at[t, 1], sems[1].at[t, 1], z_prev)

    def spread(t, n):
        pass_on(t, foreign[n], piece(seed), a1, (t, n, 0), a_next)
        pass_on(t, foreign[n], piece(seed), a1, (t, n, 1), a_prev)

    def step_z(t):
        first_z(t, piece(seed), z1)

    def step_b(t, n):
        peer, other = ((z_prev, z_next), (z_next, z_prev))[n]
        await_(t, foreign[n], piece(seed), z1, (t, n), peer)
        pass_on(t, foreign[n], part(seed, n, t % 2), z2, (t, n), other)
        spread(t, n)

    def step_c(t):
        await_(t, q_far, part(seed, 0, t % 2), z2, (t, 0), z_prev)
        await_(t, q_far, part(seed, 1, t % 2), z2, (t, 1), z_next)
        spread(t, 2)

    def step_s(t):
        first_z(t, straight(), s1)

    def step_t(t):
        await_(t, q_prev, straight(), s1, (t, 0), z_prev)
        pass_on(t, q_prev, straight(0), s2, (t, 0), z_next)
        await_(t, q_next, straight(), s1, (t, 1), z_next)
        pass_on(t, q_next, straight(1), s2, (t, 1), z_prev)

    def step_u(t):
        await_(t, q_far, straight(0), s2, (t, 0), z_prev)
        await_(t, q_far, straight(1), s2, (t, 1), z_next)

    def step_d(t, n):
        q, odd = foreign[n], (t + n) % 2
        await_(t, q, piece(seed_prev), a1, (t, n, 0), a_prev)
        pass_on(t, q, part(seed_prev, 0, odd), a2, (t, n, 0), a_next)
        await_(t, q, piece(seed_next), a1, (t, n, 1), a_next)
        pass_on(t, q, part(seed_next, 1, odd), a2, (t, n, 1), a_prev)

    def step_e(t, n):
        q, odd = foreign[n], (t + n) % 2
        await_(t, q, part(seed_far, 0, odd), a2, (t, n, 0), a_prev)
        await_(t, q, part(seed_far, 1, odd), a2, (t, n, 1), a_next)
        pass_on(t, q, pl.ds(core * SIDE, SIDE), tw, (t, n), twin)

    def step_f(t, n):
        await_(t, foreign[n], pl.ds((1 - core) * SIDE, SIDE), tw, (t, n), twin)

    head_copy = pltpu.make_async_copy(head, headbuf, lsem.at[6])
    head_copy.start()
    gain_copy = pltpu.make_async_copy(gain, gainbuf, lsem.at[7])
    gain_copy.start()
    lab_copies = [
        pltpu.make_async_copy(lab.at[:, :, cols], labels.at[:, cb], labsem.at[cb]) for cb, cols in enumerate(blocks)
    ]
    mine = [
        pltpu.make_async_copy((up, down)[t % 2].at[t // 2], wts.at[t // 2, t % 2, gy], lsem.at[9 + t]) for t in range(4)
    ]

    corner = []
    for n, plane in enumerate((0, 17)):
        corner.append(remote(pad.at[plane, :, pl.ds(128, 8)], pad.at[plane, :, above], cs.at[n, 0], cr.at[n, 0], z_next))
        corner.append(remote(pad.at[plane, :, pl.ds(8, 8)], pad.at[plane, :, below], cs.at[n, 1], cr.at[n, 1], z_prev))

    def step_h(which):
        if which == 0:
            for cb in range(4):
                landed(pad.at[0, cb, body], hs.at[0, cb], hr.at[0, cb], g_prev)
                landed(pad.at[17, cb, body], hs.at[1, cb], hr.at[1, cb], g_next)
            for copy in corner:
                copy.start()
        if which == 1:
            for cb in range(4):
                landed(edge.at[0, cb], hs.at[2, cb], hr.at[2, cb], z_prev)
                landed(edge.at[1, cb], hs.at[3, cb], hr.at[3, cb], z_next)
            keep_above, keep_below = (gy > 0).astype(F32), (gy < 3).astype(F32)
            for cb in range(4):
                for d in range(16):
                    pad[1 + d, cb, pl.ds(7, 1)] = edge[0, cb, pl.ds(d, 1)] * keep_above
                    pad[1 + d, cb, pl.ds(136, 1)] = edge[1, cb, pl.ds(d, 1)] * keep_below
        if which == 2:
            for copy in corner:
                copy.wait()

            @pl.when(gz == 0)
            def _():
                pad[0] = jnp.zeros((4, 144, 128), F32)

            @pl.when(gz == 31)
            def _():
                pad[17] = jnp.zeros((4, 144, 128), F32)

            for plane in (0, 17):
                @pl.when(gy == 0)
                def _():
                    pad[plane, :, above] = jnp.zeros((4, 8, 128), F32)

                @pl.when(gy == 3)
                def _():
                    pad[plane, :, below] = jnp.zeros((4, 8, 128), F32)

    xacc[...] = jnp.zeros_like(xacc)
    lane = lax.broadcasted_iota(jnp.int32, (8, 512), 1)
    not_first, not_last = lane != 0, lane != 511
    block = lax.broadcasted_iota(jnp.int32, (8, 128), 1) // 16
    low = {bit: (block // bit) % 2 == 0 for bit in (1, 2, 4)}

    tap = {at: jnp.full((8, 128), taps[at], F32) for at in itertools.product(range(3), repeat=3)}

    def stem_rows(d, first_row, many=8):
        totals = [[[None] * 4 for third in range(3)] for _ in range(many)]
        for first in range(3):
            for row in range(many + 2):
                for cb in range(4):
                    x = pad[d + first, cb, pl.ds(7 + first_row + row, 8, stride=16), :]
                    for second in range(3):
                        if 0 <= row - second < many:
                            mine_ = totals[row - second]
                            for third in range(3):
                                term = tap[first, second, third] * x
                                mine_[third][cb] = term if mine_[third][cb] is None else mine_[third][cb] + term
        for n in range(many):
            total = [jnp.concatenate(blocks_, axis=1) for blocks_ in totals[n]]
            left = jnp.where(not_first, pltpu.roll(total[0], 1, 1), 0.0)
            right = jnp.where(not_last, pltpu.roll(total[2], 511, 1), 0.0)
            v = 0.5 * (total[1] + left + right)
            v = v + v * jnp.tanh(v)
            stem[d, first_row + n] = v.astype(BF16).astype(F32)

    def stem_plane(d, at):
        @pl.loop(0, 2)
        def _(n):
            stem_rows(d, n * 8)

        for upper in range(2):
            for cb in range(4):
                v = [stem[d, upper * 8 + i, :, pl.ds(cb * 128, 128)] for i in range(8)]
                for bit in (1, 2, 4):
                    for i in range(8):
                        if i & bit == 0:
                            a, b = v[i], v[i + bit]
                            v[i] = jnp.where(low[bit], a, pltpu.roll(b, bit * 16, 1))
                            v[i + bit] = jnp.where(low[bit], pltpu.roll(a, 128 - bit * 16, 1), b)
                for m in range(4):
                    pair = jnp.concatenate([v[2 * m], v[2 * m + 1]], axis=0).astype(BF16)
                    cols = pl.ds(pl.multiple_of(at * 256 + upper * 128, 128), 128)
                    lhs[pl.ds(cb * 64 + m * 16, 16), cols] = pair

    def step_p(k):
        if k % 4 == 0 and k < 12:
            volume_wait(k // 4)
        if k == 8:
            volume_wait(3)
        stem_plane(groups[k // 4] + k % 4, k % 4)

    def step_g(g):
        embed_copy(g).wait()
        xacc[...] += jnp.dot(lhs[...], embuf[g % 2], preferred_element_type=F32)
        if g < 2:
            embed_copy(g + 2).start()
            mine[2 * g].start()
            mine[2 * g + 1].start()
        if g == 1:
            for copy in lab_copies:
                copy.start()

    def as_stored(x):
        return x.astype(BF16).astype(F32)

    def step_n(layer):
        if layer == 0:
            gain_copy.wait()
            for t in range(4):
                mine[t].wait()

        @pl.loop(0, 8)
        def _(n):
            at = pl.ds(pl.multiple_of(n * 32, 32), 32)
            x = as_stored(xacc[at])
            xacc[at] = x
            centred = x - jnp.mean(x, -1, keepdims=True)
            variance = jnp.mean(centred * centred, -1, keepdims=True)
            xn[at] = (centred * lax.rsqrt(variance + EPS) * gainbuf[pl.ds(layer, 1)]).astype(BF16)

    quarters = (*foreign, gy)

    def step_up(layer, n):
        u = jnp.dot(xn[...], wts[layer, 0, quarters[n]], preferred_element_type=F32)
        hid[n] = jax.nn.gelu(u, approximate=True).astype(BF16)

    def step_down(layer, n):
        xacc[...] += jnp.dot(hid[n], wts[layer, 1, quarters[n]], preferred_element_type=F32)

    def step_x():
        at_row = lax.broadcasted_iota(jnp.int32, (256, 512), 0) // 8
        at_col = lax.broadcasted_iota(jnp.int32, (256, 512), 1)
        for e in range(4):
            hit = jnp.logical_and(at_col // 16 == at_row, (at_col // 4) % 4 == e)
            expand[pl.ds(e * 256, 256)] = hit.astype(F32).astype(BF16)

    def step_k(cb):
        if cb == 0:
            for copy in lab_copies:
                copy.wait()

        def row_step(d, carry):
            carry = list(carry)
            for i in range(16):
                l = labels[d, cb, pl.ds(i, 8, stride=16), :]
                for c in range(4):
                    carry[c] = carry[c] + jnp.where(l == c, 1.0, 0.0)
            return tuple(carry)

        final = lax.fori_loop(0, 16, row_step, (jnp.zeros((8, 128), F32),) * 4)
        for c in range(4):
            sums[pl.ds(64 + c * 8, 8), blocks[cb]] = final[c]

    doing = {
        "z": step_z, "b": step_b, "c": step_c, "s": step_s, "t": step_t, "u": step_u, "d": step_d, "e": step_e, "f": step_f,
        "h": step_h, "p": step_p, "g": step_g, "n": step_n, "U": step_up, "D": step_down, "x": step_x, "k": step_k,
    }
    plan = [
        ('z', 0), ('z', 1), ('s', 0), ('h', 1), ('p', 0), ('b', 0, 0), ('b', 0, 1), ('z', 2),
        ('s', 1), ('p', 1), ('p', 2), ('p', 3), ('b', 1, 0), ('b', 1, 1), ('z', 3), ('s', 2),
        ('g', 0), ('t', 0), ('h', 0), ('d', 0, 0), ('p', 4), ('c', 0), ('p', 5), ('d', 0, 1),
        ('p', 6), ('p', 7), ('d', 1, 0), ('b', 2, 0), ('b', 2, 1), ('z', 4), ('s', 3), ('d', 1, 1),
        ('t', 1), ('g', 1), ('e', 0, 0), ('p', 8), ('c', 1), ('d', 0, 2), ('p', 9), ('e', 0, 1),
        ('h', 2), ('e', 1, 0), ('p', 10), ('b', 3, 0), ('b', 3, 1), ('z', 5), ('s', 4), ('d', 2, 0),
        ('p', 11), ('f', 0, 0), ('t', 2), ('d', 2, 1), ('g', 2), ('u', 0), ('e', 1, 1), ('p', 12),
        ('f', 0, 1), ('c', 2), ('d', 1, 2), ('f', 1, 0), ('p', 13), ('e', 0, 2), ('p', 14), ('d', 3, 0),
        ('b', 4, 0), ('b', 4, 1), ('z', 6), ('s', 5), ('p', 15), ('d', 3, 1), ('f', 1, 1), ('t', 3),
        ('e', 2, 0), ('g', 3), ('u', 1), ('e', 2, 1), ('n', 0), ('f', 0, 2), ('U', 0, 3), ('c', 3),
        ('d', 2, 2), ('e', 1, 2), ('x',), ('e', 3, 0), ('k', 0), ('f', 2, 0), ('b', 5, 0), ('b', 5, 1),
        ('z', 7), ('s', 6), ('d', 4, 0), ('f', 2, 1), ('k', 1), ('d', 4, 1), ('t', 4), ('e', 3, 1),
        ('k', 2), ('u', 2), ('f', 1, 2), ('k', 3), ('d', 3, 2), ('f', 3, 0), ('c', 4), ('e', 2, 2),
        ('U', 0, 0), ('d', 5, 0), ('U', 0, 1), ('f', 3, 1), ('b', 6, 0), ('b', 6, 1), ('d', 5, 1), ('U', 0, 2),
        ('e', 4, 0), ('t', 5), ('e', 4, 1), ('D', 0, 3), ('f', 2, 2), ('u', 3), ('e', 3, 2), ('D', 0, 0),
        ('D', 0, 1), ('c', 5), ('d', 4, 2), ('e', 5, 0), ('d', 6, 0), ('f', 4, 0), ('b', 7, 0), ('b', 7, 1),
        ('s', 7), ('f', 4, 1), ('d', 6, 1), ('f', 3, 2), ('D', 0, 2), ('e', 5, 1), ('t', 6), ('n', 1),
        ('u', 4), ('f', 5, 0), ('d', 5, 2), ('U', 1, 3), ('e', 4, 2), ('c', 6), ('e', 6, 0), ('u', 5),
        ('U', 1, 0), ('d', 7, 0), ('c', 7), ('f', 5, 1), ('U', 1, 1), ('d', 7, 1), ('t', 7), ('e', 6, 1),
        ('u', 6), ('e', 5, 2), ('f', 4, 2), ('f', 6, 0), ('d', 6, 2), ('e', 7, 0), ('u', 7), ('d', 7, 2),
        ('f', 6, 1), ('e', 7, 1), ('f', 5, 2), ('U', 1, 2), ('e', 6, 2), ('D', 1, 3), ('f', 7, 0), ('D', 1, 0),
        ('e', 7, 2), ('f', 7, 1), ('D', 1, 1), ('f', 6, 2), ('f', 7, 2), ('D', 1, 2),
    ]
    for name, *args in plan:
        doing[name](*args)

    head_copy.wait()
    token = lax.broadcasted_iota(jnp.int32, (256, 256), 0)
    patch = (token % 8) * 32 + token // 8
    listed = jnp.max((slots[0] == patch).astype(F32), axis=1, keepdims=True)
    q = jnp.dot(xacc[...].astype(BF16), headbuf[...], preferred_element_type=F32)
    q = (as_stored(q) * listed).T
    coarse[0] = q[:, :128]
    coarse[1] = q[:, 128:]
    token = lax.broadcasted_iota(jnp.int32, (8, 256), 1)
    own_row = (token % 8 == lax.broadcasted_iota(jnp.int32, (8, 256), 0)).astype(F32)

    for c in range(4):
        spread_q = []
        for e in range(4):
            at = pl.ds(c * 64 + e, 16, stride=4)
            part = jnp.concatenate([coarse[0, at, :], coarse[1, at, :]], axis=1)
            spread_q.append((part[:, None, :] * own_row[None]).reshape(128, 256).astype(BF16))
        u = jnp.zeros((128, 512), F32)
        for e in range(4):
            u = u + jnp.dot(spread_q[e], expand[pl.ds(e * 256, 256)], preferred_element_type=F32)
        upq[pl.ds(c * 128, 128)] = 0.5 * (u + bias[c])
    half_skip = [0.5 * skip[c] for c in range(4)]
    for cb in range(4):
        cols = pl.ds(cb * 128, 128)

        def block_step(ab, carry):
            carry = list(carry)
            a, b = lax.div(ab, 4), lax.rem(ab, 4)
            level = [upq[pl.ds(pl.multiple_of(c * 128 + ab * 8, 8), 8), cols] for c in range(4)]
            for dd in range(4):
                for ii in range(4):
                    d, i = a * 4 + dd, b * 4 + ii
                    s = stem[d, i, :, cols]
                    l = labels[d, cb, pl.ds(i, 8, stride=16), :]
                    for c in range(4):
                        t = jnp.tanh(level[c] + half_skip[c] * s)
                        carry[c] = carry[c] + t
                        match = l == c
                        carry[4 + c] = carry[4 + c] + jnp.where(match, t, 0.0)
            return tuple(carry)

        final = lax.fori_loop(0, 16, block_step, (jnp.zeros((8, 128), F32),) * 8)
        for c in range(4):
            sums[pl.ds(c * 8, 8), cols] = 0.5 * (final[4 + c] + sums[pl.ds(64 + c * 8, 8), cols])
            sums[pl.ds(32 + c * 8, 8), cols] = 8 * 16 + 0.5 * final[c]

    fold = lax.broadcasted_iota(jnp.int32, (512, 256), 0) // 16 == lax.broadcasted_iota(jnp.int32, (512, 256), 1) % 32
    folded = jnp.dot(sums[...], fold.astype(F32), preferred_element_type=F32, precision=lax.Precision.HIGHEST)
    here = lax.broadcasted_iota(jnp.int32, (8, 256), 1) // 32 == lax.broadcasted_iota(jnp.int32, (8, 256), 0)
    lines = [
        jnp.sum(jnp.where(here, folded[n * 8 : n * 8 + 8], 0.0), axis=0, keepdims=True) for n in range(12)
    ]
    inter, mass, count = (jnp.concatenate(lines[n * 4 : n * 4 + 4], axis=0) for n in range(3))
    out[0, 0] = (2.0 * inter + 1.0) / (mass + count + 1.0)

    def send_line(x):
        return jnp.broadcast_to(jnp.sum(x, axis=1, keepdims=True), (4, 128))

    inbox[0] = jnp.concatenate(
        [send_line(inter), send_line(mass), send_line(count), jnp.zeros((4, 128), F32)], axis=0
    )
    for n, peer in inner_group:
        send(inbox.at[0], inbox.at[n], ps.at[n], pr.at[n], peer)
    for n, peer in inner_group:
        landed(inbox.at[n], ps.at[n], pr.at[n], peer)
    total = inbox[0]
    for n in range(1, 8):
        total = total + inbox[n]
    outbox[0] = total
    for n, peer in outer_group:
        send(outbox.at[0], outbox.at[n], ps.at[7 + n], pr.at[7 + n], peer)
    for n, peer in outer_group:
        landed(outbox.at[n], ps.at[7 + n], pr.at[7 + n], peer)
    for n in range(1, 16):
        total = total + outbox[n]
    ratio = (2.0 * total[0:4] + 1.0) / (total[4:8] + total[8:12] + 1.0)
    for c in range(4):
        dice[c] = ratio[c, 0]

    for copy in sent:
        copy.wait_send()


def per_device(
    volume, labels, patch_list, stem_kernel, embed_weight, norm_gain, up_weight, down_weight, head_weight, skip_weight, class_bias
):
    hbm = pl.BlockSpec(memory_space=pl.ANY)
    smem = pl.BlockSpec(memory_space=pltpu.SMEM)
    vmem = pl.BlockSpec(memory_space=pltpu.VMEM)
    dma = pltpu.SemaphoreType.DMA
    return pl.pallas_call(
        kernel,
        out_shape=(jax.ShapeDtypeStruct((1, 1, 4, 256), F32), jax.ShapeDtypeStruct((4,), F32)),
        in_specs=[hbm, hbm, vmem, smem, hbm, hbm, hbm, hbm, hbm, smem, smem],
        out_specs=(vmem, smem),
        scratch_shapes=[
            pltpu.VMEM((18, 4, 144, 128), F32),
            pltpu.VMEM((2, 2, 4, 1024, 1024), BF16),
            pltpu.VMEM((2, 1024, 1024), BF16),
            pltpu.VMEM((16, 16, 8, 512), F32),
            pltpu.VMEM((16, 4, 128, 128), jnp.int32),
            pltpu.VMEM((256, 1024), BF16),
            pltpu.VMEM((256, 1024), F32),
            pltpu.VMEM((256, 1024), BF16),
            pltpu.VMEM((4, 256, 1024), BF16),
            pltpu.VMEM((2, 256, 128), F32),
            pltpu.VMEM((512, 512), F32),
            pltpu.VMEM((1024, 512), BF16),
            pltpu.VMEM((96, 512), F32),
            pltpu.VMEM((1024, 256), BF16),
            pltpu.VMEM((2, 1024), F32),
            pltpu.VMEM((2, 4, 16, 128), F32),
            pltpu.VMEM((8, 16, 128), F32),
            pltpu.VMEM((16, 16, 128), F32),
            dma((4, 4)), dma((4, 4)), dma((2, 2)), dma((2, 2)), dma((4, 4)), dma((4,)),
            dma((8, 2)), dma((8, 2)), dma((8, 2)), dma((8, 2)),
            dma((8, 2)), dma((8, 2)), dma((8, 2)), dma((8, 2)),
            dma((8, 3, 2)), dma((8, 3, 2)), dma((8, 3, 2)), dma((8, 3, 2)),
            dma((8, 3)), dma((8, 3)),
            dma((23,)), dma((23,)),
            dma((13,)),
        ],
        compiler_params=pltpu.CompilerParams(
            collective_id=0, has_side_effects=True, vmem_limit_bytes=60 * 1024 * 1024
        ),
    )(
        volume, labels, patch_list, stem_kernel, embed_weight, norm_gain,
        up_weight, down_weight, head_weight, skip_weight, class_bias,
    )


def solution(mesh):
    placed = (
        P("gz", "gy", None),
        P("gz", "gy", None),
        P("gz", "gy", None),
        P(),
        P(),
        P(),
        P(None, None, "gy"),
        P(None, "gy", None),
        P(),
        P(),
        P(),
    )
    return jax.shard_map(
        per_device,
        mesh=mesh,
        in_specs=placed,
        out_specs=(P("gz", "gy", None, None), P()),
        check_vma=False,
    )
```

```python
import itertools

import jax
import jax.numpy as jnp
from jax import lax
from jax.experimental import pallas as pl
from jax.experimental.pallas import tpu as pltpu
from jax.sharding import PartitionSpec as P

EPS = 1e-05
MESH = pl.DeviceIdType.MESH
F32 = jnp.float32
BF16 = jnp.bfloat16

SIDE, PIECE, STRAIGHT = 512, 112, 64
STAGES = ((0, 0, 0, 512), (0, 0, 512, 512), (0, 1, 0, 512), (0, 1, 512, 512), (1, 0, 0, 512), (1, 0, 512, 512), (1, 1, 0, 256))


def kernel(
    vol, lab, slots, taps, emb, gain, up, down, head, skip, bias,
    out, dice,
    pad, wts, embuf, stem, labels, lhs, xacc, xn, hid, coarse, upq, expand, sums, headbuf, gainbuf, edge, cacc, inbox, outbox,
    hs, hr, cs, cr, vsem, labsem, z1s, z1r, z2s, z2r, s1s, s1r, s2s, s2r, a1s, a1r, a2s, a2r, tws, twr, ps, pr, lsem,
):
    gz, gy = lax.axis_index("gz"), lax.axis_index("gy")
    core = lax.rem(gz, 2)
    chip = lax.div(gz, 2)
    cx, cy = lax.rem(chip, 4), lax.div(chip, 4)
    seed = (1 - core) * cx + core * cy

    def along(step):
        first = (cy * 4 + lax.rem(cx + step, 4)) * 2
        second = (lax.rem(cy + step, 4) * 4 + cx) * 2 + 1
        return ((1 - core) * first + core * second, gy)

    z_next, z_prev = (gz, lax.rem(gy + 1, 4)), (gz, lax.rem(gy + 3, 4))
    a_next, a_prev = along(1), along(3)
    g_next, g_prev = (lax.rem(gz + 1, 32), gy), (lax.rem(gz + 31, 32), gy)
    twin = (gz + 1 - 2 * core, gy)
    q_prev, q_next, q_far = lax.rem(gy + 3, 4), lax.rem(gy + 1, 4), lax.rem(gy + 2, 4)
    foreign = (q_prev, q_next, q_far)

    inner_group = [(n, (chip * 2 + lax.rem(core + n // 4, 2), lax.rem(gy + n % 4, 4))) for n in range(1, 8)]
    outer_group = [
        (n, ((lax.rem(cy + n // 4, 4) * 4 + lax.rem(cx + n % 4, 4)) * 2 + core, gy)) for n in range(1, 16)
    ]
    crossing = (lax.rem(gz + 31 + 2 * core, 32), gy)

    body, inner = pl.ds(8, 128), pl.ds(1, 16)
    above, below = pl.ds(0, 8), pl.ds(136, 8)
    blocks = [pl.ds(cb * 128, 128) for cb in range(4)]
    groups = (4, 8, 12, 0)
    local = []
    parts = ((3, 6), (9, 4), (13, 3), (0, 3))
    for n, (first, many) in enumerate(parts):
        for cb, cols in enumerate(blocks):
            copy = pltpu.make_async_copy(
                vol.at[pl.ds(first, many), :, cols], pad.at[pl.ds(1 + first, many), cb, body], vsem.at[n, cb]
            )
            copy.start()
            local.append(copy)

    def volume_wait(n):
        for copy in local[n * 4 : n * 4 + 4]:
            copy.wait()

    def embed_copy(g):
        return pltpu.make_async_copy(
            emb.at[pl.ds(groups[g] * 256, 1024)], embuf.at[g % 2], lsem.at[4 + g % 2]
        )

    mine = [
        pltpu.make_async_copy((up, down)[t % 2].at[t // 2], wts.at[t // 2, t % 2, gy], lsem.at[9 + t]) for t in range(4)
    ]
    head_copy = pltpu.make_async_copy(head, headbuf, lsem.at[6])
    head_copy.start()
    mine[3].start()
    embed_copy(0).start()
    embed_copy(1).start()

    barrier = pltpu.get_barrier_semaphore()
    for _, peer in inner_group + outer_group + [(0, crossing)]:
        pl.semaphore_signal(barrier, inc=1, device_id=peer, device_id_type=MESH)
    pl.semaphore_wait(barrier, 23)

    def remote(src, dst, send, recv, peer):
        return pltpu.make_async_remote_copy(
            src_ref=src, dst_ref=dst, send_sem=send, recv_sem=recv, device_id=peer, device_id_type=MESH
        )

    z1, z2, s1, s2, a1, a2, tw = (z1s, z1r), (z2s, z2r), (s1s, s1r), (s2s, s2r), (a1s, a1r), (a2s, a2r), (tws, twr)
    sent = []

    def send(*args):
        copy = remote(*args)
        copy.start()
        sent.append(copy)

    def landed(dst, send_sem, recv_sem, peer):
        remote(dst, dst, send_sem, recv_sem, peer).wait_recv()

    for cb, cols in enumerate(blocks):
        send(vol.at[:, 127, cols], edge.at[0, cb], hs.at[2, cb], hr.at[2, cb], z_next)
        send(vol.at[:, 0, cols], edge.at[1, cb], hs.at[3, cb], hr.at[3, cb], z_prev)
    for cb, cols in enumerate(blocks):
        send(vol.at[15, :, cols], pad.at[0, cb, body], hs.at[0, cb], hr.at[0, cb], g_next)
        send(vol.at[0, :, cols], pad.at[17, cb, body], hs.at[1, cb], hr.at[1, cb], g_prev)

    def view(t, q, at):
        layer, matrix, first, width = STAGES[t]
        return wts.at[layer, matrix, q, at, pl.ds(first, width)]

    def own(t, at):
        layer, matrix, first, width = STAGES[t]
        if (layer, matrix) == (1, 1):
            return wts.at[layer, matrix, gy, at, pl.ds(first, width)]
        return (up, down)[matrix].at[layer, at, pl.ds(first, width)]

    seed_prev, seed_next, seed_far = lax.rem(seed + 3, 4), lax.rem(seed + 1, 4), lax.rem(seed + 2, 4)

    def piece(at):
        return pl.ds(core * SIDE + at * PIECE, PIECE)

    def part(at, h, odd):
        first = 48 if odd else 64
        return pl.ds(core * SIDE + at * PIECE + h * first, PIECE - first if h else first)

    def straight(h=None):
        if h is None:
            return pl.ds(core * SIDE + 4 * PIECE, STRAIGHT)
        return pl.ds(core * SIDE + 4 * PIECE + h * (STRAIGHT // 2), STRAIGHT // 2)

    def pass_on(t, q, at, sems, index, peer):
        send(view(t, q, at), view(t, q, at), sems[0].at[index], sems[1].at[index], peer)

    def await_(t, q, at, sems, index, peer):
        landed(view(t, q, at), sems[0].at[index], sems[1].at[index], peer)

    def first_z(t, at, sems):
        send(own(t, at), view(t, gy, at), sems[0].at[t, 0], sems[1].at[t, 0], z_next)
        send(own(t, at), view(t, gy, at), sems[0].at[t, 1], sems[1].at[t, 1], z_prev)

    def spread(t, n):
        pass_on(t, foreign[n], piece(seed), a1, (t, n, 0), a_next)
        pass_on(t, foreign[n], piece(seed), a1, (t, n, 1), a_prev)

    def step_z(t):
        first_z(t, piece(seed), z1)

    def step_b(t, n):
        peer, other = ((z_prev, z_next), (z_next, z_prev))[n]
        await_(t, foreign[n], piece(seed), z1, (t, n), peer)
        pass_on(t, foreign[n], part(seed, n, t % 2), z2, (t, n), other)
        spread(t, n)

    def step_c(t):
        await_(t, q_far, part(seed, 0, t % 2), z2, (t, 0), z_prev)
        await_(t, q_far, part(seed, 1, t % 2), z2, (t, 1), z_next)
        spread(t, 2)

    def step_s(t):
        first_z(t, straight(), s1)

    def step_t(t):
        await_(t, q_prev, straight(), s1, (t, 0), z_prev)
        pass_on(t, q_prev, straight(0), s2, (t, 0), z_next)
        await_(t, q_next, straight(), s1, (t, 1), z_next)
        pass_on(t, q_next, straight(1), s2, (t, 1), z_prev)

    def step_u(t):
        await_(t, q_far, straight(0), s2, (t, 0), z_prev)
        await_(t, q_far, straight(1), s2, (t, 1), z_next)

    def step_d(t, n):
        q, odd = foreign[n], (t + n) % 2
        await_(t, q, piece(seed_prev), a1, (t, n, 0), a_prev)
        pass_on(t, q, part(seed_prev, 0, odd), a2, (t, n, 0), a_next)
        await_(t, q, piece(seed_next), a1, (t, n, 1), a_next)
        pass_on(t, q, part(seed_next, 1, odd), a2, (t, n, 1), a_prev)

    def step_e(t, n):
        q, odd = foreign[n], (t + n) % 2
        await_(t, q, part(seed_far, 0, odd), a2, (t, n, 0), a_prev)
        await_(t, q, part(seed_far, 1, odd), a2, (t, n, 1), a_next)
        pass_on(t, q, pl.ds(core * SIDE, SIDE), tw, (t, n), twin)

    def step_f(t, n):
        await_(t, foreign[n], pl.ds((1 - core) * SIDE, SIDE), tw, (t, n), twin)

    gain_copy = pltpu.make_async_copy(gain, gainbuf, lsem.at[7])
    gain_copy.start()
    lab_copies = [
        pltpu.make_async_copy(lab.at[:, :, cols], labels.at[:, cb], labsem.at[cb]) for cb, cols in enumerate(blocks)
    ]
    corner = []
    for n, plane in enumerate((0, 17)):
        corner.append(remote(pad.at[plane, :, pl.ds(128, 8)], pad.at[plane, :, above], cs.at[n, 0], cr.at[n, 0], z_next))
        corner.append(remote(pad.at[plane, :, pl.ds(8, 8)], pad.at[plane, :, below], cs.at[n, 1], cr.at[n, 1], z_prev))

    def step_h(which):
        if which == 0:
            for cb in range(4):
                landed(pad.at[0, cb, body], hs.at[0, cb], hr.at[0, cb], g_prev)
                landed(pad.at[17, cb, body], hs.at[1, cb], hr.at[1, cb], g_next)
            for copy in corner:
                copy.start()
        if which == 1:
            for cb in range(4):
                landed(edge.at[0, cb], hs.at[2, cb], hr.at[2, cb], z_prev)
                landed(edge.at[1, cb], hs.at[3, cb], hr.at[3, cb], z_next)
            keep_above, keep_below = (gy > 0).astype(F32), (gy < 3).astype(F32)
            for cb in range(4):
                for d in range(16):
                    pad[1 + d, cb, pl.ds(7, 1)] = edge[0, cb, pl.ds(d, 1)] * keep_above
                    pad[1 + d, cb, pl.ds(136, 1)] = edge[1, cb, pl.ds(d, 1)] * keep_below
        if which == 2:
            for copy in corner:
                copy.wait()

            @pl.when(gz == 0)
            def _():
                pad[0] = jnp.zeros((4, 144, 128), F32)

            @pl.when(gz == 31)
            def _():
                pad[17] = jnp.zeros((4, 144, 128), F32)

            for plane in (0, 17):
                @pl.when(gy == 0)
                def _():
                    pad[plane, :, above] = jnp.zeros((4, 8, 128), F32)

                @pl.when(gy == 3)
                def _():
                    pad[plane, :, below] = jnp.zeros((4, 8, 128), F32)

    xacc[...] = jnp.zeros_like(xacc)
    lane = lax.broadcasted_iota(jnp.int32, (8, 512), 1)
    not_first, not_last = lane != 0, lane != 511
    block = lax.broadcasted_iota(jnp.int32, (8, 128), 1) // 16
    low = {bit: (block // bit) % 2 == 0 for bit in (1, 2, 4)}

    tap = {at: jnp.full((8, 128), taps[at], F32) for at in itertools.product(range(3), repeat=3)}

    def stem_rows(d, first_row, many=8):
        totals = [[[None] * 4 for third in range(3)] for _ in range(many)]
        for first in range(3):
            for row in range(many + 2):
                for cb in range(4):
                    x = pad[d + first, cb, pl.ds(7 + first_row + row, 8, stride=16), :]
                    for second in range(3):
                        if 0 <= row - second < many:
                            mine_ = totals[row - second]
                            for third in range(3):
                                term = tap[first, second, third] * x
                                mine_[third][cb] = term if mine_[third][cb] is None else mine_[third][cb] + term
        for n in range(many):
            total = [jnp.concatenate(blocks_, axis=1) for blocks_ in totals[n]]
            left = jnp.where(not_first, pltpu.roll(total[0], 1, 1), 0.0)
            right = jnp.where(not_last, pltpu.roll(total[2], 511, 1), 0.0)
            v = 0.5 * (total[1] + left + right)
            v = v + v * jnp.tanh(v)
            stem[d, first_row + n] = v.astype(BF16).astype(F32)

    def stem_plane(d, at):
        @pl.loop(0, 2)
        def _(n):
            stem_rows(d, n * 8)

        for upper in range(2):
            for cb in range(4):
                v = [stem[d, upper * 8 + i, :, pl.ds(cb * 128, 128)] for i in range(8)]
                for bit in (1, 2, 4):
                    for i in range(8):
                        if i & bit == 0:
                            a, b = v[i], v[i + bit]
                            v[i] = jnp.where(low[bit], a, pltpu.roll(b, bit * 16, 1))
                            v[i + bit] = jnp.where(low[bit], pltpu.roll(a, 128 - bit * 16, 1), b)
                for m in range(4):
                    pair = jnp.concatenate([v[2 * m], v[2 * m + 1]], axis=0).astype(BF16)
                    cols = pl.ds(pl.multiple_of(at * 256 + upper * 128, 128), 128)
                    lhs[pl.ds(cb * 64 + m * 16, 16), cols] = pair

    def step_p(k):
        if k % 4 == 0 and k < 12:
            volume_wait(k // 4)
        if k == 8:
            volume_wait(3)
        stem_plane(groups[k // 4] + k % 4, k % 4)

    def step_g(g):
        embed_copy(g).wait()
        xacc[...] += jnp.dot(lhs[...], embuf[g % 2], preferred_element_type=F32)
        if g < 2:
            embed_copy(g + 2).start()
            mine[2 * g].start()
        if g == 0:
            mine[1].start()
        if g == 1:
            for copy in lab_copies:
                copy.start()

    def as_stored(x):
        return x.astype(BF16).astype(F32)

    def step_n(layer):
        if layer == 0:
            gain_copy.wait()
            for t in range(3):
                mine[t].wait()

        @pl.loop(0, 8)
        def _(n):
            at = pl.ds(pl.multiple_of(n * 32, 32), 32)
            x = as_stored(xacc[at])
            xacc[at] = x
            centred = x - jnp.mean(x, -1, keepdims=True)
            variance = jnp.mean(centred * centred, -1, keepdims=True)
            xn[at] = (centred * lax.rsqrt(variance + EPS) * gainbuf[pl.ds(layer, 1)]).astype(BF16)

        if layer == 1:
            cacc[...] = jnp.dot(xacc[...].astype(BF16), headbuf[...], preferred_element_type=F32)

    quarters = (*foreign, gy)

    def step_up(layer, n):
        u = jnp.dot(xn[...], wts[layer, 0, quarters[n]], preferred_element_type=F32)
        hid[n] = jax.nn.gelu(u, approximate=True).astype(BF16)

    def step_w():
        mine[3].wait()
        head_copy.wait()
        folded_rows = jnp.dot(wts[1, 1, gy], headbuf[...], preferred_element_type=F32)
        wts[1, 1, gy, :, pl.ds(0, 256)] = folded_rows.astype(BF16)

    def step_down(layer, n):
        if layer == 1:
            cacc[...] += jnp.dot(hid[n], wts[1, 1, quarters[n], :, pl.ds(0, 256)], preferred_element_type=F32)
            return
        xacc[...] += jnp.dot(hid[n], wts[layer, 1, quarters[n]], preferred_element_type=F32)

    def step_x():
        at_row = lax.broadcasted_iota(jnp.int32, (256, 512), 0) // 8
        at_col = lax.broadcasted_iota(jnp.int32, (256, 512), 1)
        for e in range(4):
            hit = jnp.logical_and(at_col // 16 == at_row, (at_col // 4) % 4 == e)
            expand[pl.ds(e * 256, 256)] = hit.astype(F32).astype(BF16)

    def step_k(cb):
        if cb == 0:
            for copy in lab_copies:
                copy.wait()

        def row_step(d, carry):
            carry = list(carry)
            for i in range(16):
                l = labels[d, cb, pl.ds(i, 8, stride=16), :]
                pad[d, cb, pl.ds(i * 8, 8)] = l.astype(F32)
                for c in range(4):
                    carry[c] = carry[c] + jnp.where(l == c, 1.0, 0.0)
            return tuple(carry)

        final = lax.fori_loop(0, 16, row_step, (jnp.zeros((8, 128), F32),) * 4)
        for c in range(4):
            sums[pl.ds(64 + c * 8, 8), blocks[cb]] = final[c]

    doing = {
        "z": step_z, "b": step_b, "c": step_c, "s": step_s, "t": step_t, "u": step_u, "d": step_d, "e": step_e, "f": step_f,
        "h": step_h, "p": step_p, "g": step_g, "n": step_n, "U": step_up, "D": step_down, "x": step_x, "w": step_w, "k": step_k,
    }
    plan = [
        ('z', 0), ('z', 1), ('w',), ('h', 1), ('p', 0), ('b', 0, 0), ('b', 0, 1), ('z', 2),
        ('s', 0), ('p', 1), ('p', 2), ('p', 3), ('b', 1, 0), ('b', 1, 1), ('z', 3), ('s', 1),
        ('g', 0), ('h', 0), ('p', 4), ('d', 0, 0), ('c', 0), ('p', 5), ('d', 0, 1), ('p', 6),
        ('b', 2, 0), ('b', 2, 1), ('z', 4), ('s', 2), ('d', 1, 0), ('p', 7), ('t', 0), ('d', 1, 1),
        ('g', 1), ('e', 0, 0), ('c', 1), ('p', 8), ('d', 0, 2), ('p', 9), ('e', 0, 1), ('h', 2),
        ('p', 10), ('b', 3, 0), ('b', 3, 1), ('z', 5), ('s', 3), ('d', 2, 0), ('p', 11), ('f', 0, 0),
        ('t', 1), ('d', 2, 1), ('e', 1, 0), ('g', 2), ('c', 2), ('e', 1, 1), ('p', 12), ('f', 0, 1),
        ('d', 1, 2), ('p', 13), ('b', 4, 0), ('b', 4, 1), ('z', 6), ('s', 4), ('p', 14), ('d', 3, 0),
        ('f', 1, 0), ('p', 15), ('t', 2), ('d', 3, 1), ('f', 1, 1), ('u', 0), ('e', 0, 2), ('e', 2, 0),
        ('g', 3), ('e', 2, 1), ('c', 3), ('n', 0), ('U', 0, 3), ('d', 2, 2), ('x',), ('b', 5, 0),
        ('b', 5, 1), ('k', 0), ('d', 4, 0), ('f', 0, 2), ('k', 1), ('t', 3), ('f', 2, 0), ('d', 4, 1),
        ('u', 1), ('e', 1, 2), ('e', 3, 0), ('f', 2, 1), ('k', 2), ('e', 3, 1), ('c', 4), ('k', 3),
        ('d', 3, 2), ('b', 6, 0), ('b', 6, 1), ('s', 5), ('s', 6), ('U', 0, 0), ('d', 5, 0), ('t', 4),
        ('U', 0, 1), ('f', 1, 2), ('u', 2), ('e', 2, 2), ('f', 3, 0), ('d', 5, 1), ('U', 0, 2), ('e', 4, 0),
        ('c', 5), ('f', 3, 1), ('e', 4, 1), ('u', 3), ('D', 0, 3), ('c', 6), ('D', 0, 0), ('d', 4, 2),
        ('e', 3, 2), ('D', 0, 1), ('t', 5), ('d', 6, 0), ('f', 2, 2), ('t', 6), ('d', 6, 1), ('u', 4),
        ('e', 5, 0), ('f', 4, 0), ('e', 5, 1), ('f', 4, 1), ('d', 5, 2), ('f', 3, 2), ('D', 0, 2), ('d', 6, 2),
        ('u', 5), ('n', 1), ('u', 6), ('e', 4, 2), ('e', 6, 0), ('e', 6, 1), ('U', 1, 3), ('f', 5, 0),
        ('U', 1, 0), ('f', 5, 1), ('e', 5, 2), ('U', 1, 1), ('e', 6, 2), ('f', 4, 2), ('f', 6, 0), ('f', 6, 1),
        ('f', 5, 2), ('U', 1, 2), ('f', 6, 2), ('D', 1, 3), ('D', 1, 0), ('D', 1, 1), ('D', 1, 2),
    ]
    for name, *args in plan:
        doing[name](*args)

    token = lax.broadcasted_iota(jnp.int32, (256, 256), 0)
    patch = (token % 8) * 32 + token // 8
    listed = jnp.max((slots[0] == patch).astype(F32), axis=1, keepdims=True)
    q = (as_stored(cacc[...]) * listed).T
    coarse[0] = q[:, :128]
    coarse[1] = q[:, 128:]
    token = lax.broadcasted_iota(jnp.int32, (8, 256), 1)
    own_row = (token % 8 == lax.broadcasted_iota(jnp.int32, (8, 256), 0)).astype(F32)

    for c in range(4):
        spread_q = []
        for e in range(4):
            at = pl.ds(c * 64 + e, 16, stride=4)
            part = jnp.concatenate([coarse[0, at, :], coarse[1, at, :]], axis=1)
            spread_q.append((part[:, None, :] * own_row[None]).reshape(128, 256).astype(BF16))
        u = jnp.zeros((128, 512), F32)
        for e in range(4):
            u = u + jnp.dot(spread_q[e], expand[pl.ds(e * 256, 256)], preferred_element_type=F32)
        upq[pl.ds(c * 128, 128)] = 0.5 * (u + bias[c])
    half_skip = [0.5 * skip[c] for c in range(4)]
    for cb in range(4):
        cols = pl.ds(cb * 128, 128)

        def block_step(ab, carry):
            carry = list(carry)
            a, b = lax.div(ab, 4), lax.rem(ab, 4)
            level = [upq[pl.ds(pl.multiple_of(c * 128 + ab * 8, 8), 8), cols] for c in range(4)]
            for dd in range(4):
                for ii in range(4):
                    d, i = a * 4 + dd, b * 4 + ii
                    s = stem[d, i, :, cols]
                    l = pad[d, cb, pl.ds(pl.multiple_of(i * 8, 8), 8)]
                    for c in range(4):
                        t = jnp.tanh(level[c] + half_skip[c] * s)
                        carry[c] = carry[c] + t
                        match = l == float(c)
                        carry[4 + c] = carry[4 + c] + jnp.where(match, t, 0.0)
            return tuple(carry)

        final = lax.fori_loop(0, 16, block_step, (jnp.zeros((8, 128), F32),) * 8)
        for c in range(4):
            sums[pl.ds(c * 8, 8), cols] = 0.5 * (final[4 + c] + sums[pl.ds(64 + c * 8, 8), cols])
            sums[pl.ds(32 + c * 8, 8), cols] = 8 * 16 + 0.5 * final[c]

    fold = lax.broadcasted_iota(jnp.int32, (512, 256), 0) // 16 == lax.broadcasted_iota(jnp.int32, (512, 256), 1) % 32
    folded = jnp.dot(sums[...], fold.astype(F32), preferred_element_type=F32, precision=lax.Precision.HIGHEST)
    here = lax.broadcasted_iota(jnp.int32, (8, 256), 1) // 32 == lax.broadcasted_iota(jnp.int32, (8, 256), 0)
    lines = [
        jnp.sum(jnp.where(here, folded[n * 8 : n * 8 + 8], 0.0), axis=0, keepdims=True) for n in range(12)
    ]
    inter, mass, count = (jnp.concatenate(lines[n * 4 : n * 4 + 4], axis=0) for n in range(3))
    def send_line(x):
        return jnp.broadcast_to(jnp.sum(x, axis=1, keepdims=True), (4, 128))

    inbox[0] = jnp.concatenate(
        [send_line(inter), send_line(mass), send_line(count), jnp.zeros((4, 128), F32)], axis=0
    )
    for n, peer in inner_group:
        send(inbox.at[0], inbox.at[n], ps.at[n], pr.at[n], peer)
    for copy in sent:
        copy.wait_send()
    sent.clear()
    out[0, 0] = (2.0 * inter + 1.0) / (mass + count + 1.0)
    for n, peer in inner_group:
        landed(inbox.at[n], ps.at[n], pr.at[n], peer)
    total = inbox[0]
    for n in range(1, 8):
        total = total + inbox[n]
    outbox[0] = total
    for n, peer in outer_group:
        send(outbox.at[0], outbox.at[n], ps.at[7 + n], pr.at[7 + n], peer)
    for n, peer in outer_group:
        landed(outbox.at[n], ps.at[7 + n], pr.at[7 + n], peer)
    for copy in sent:
        copy.wait_send()
    for n in range(1, 16):
        total = total + outbox[n]
    ratio = (2.0 * total[0:4] + 1.0) / (total[4:8] + total[8:12] + 1.0)
    for c in range(4):
        dice[c] = ratio[c, 0]


def per_device(
    volume, labels, patch_list, stem_kernel, embed_weight, norm_gain, up_weight, down_weight, head_weight, skip_weight, class_bias
):
    hbm = pl.BlockSpec(memory_space=pl.ANY)
    smem = pl.BlockSpec(memory_space=pltpu.SMEM)
    vmem = pl.BlockSpec(memory_space=pltpu.VMEM)
    dma = pltpu.SemaphoreType.DMA
    return pl.pallas_call(
        kernel,
        out_shape=(jax.ShapeDtypeStruct((1, 1, 4, 256), F32), jax.ShapeDtypeStruct((4,), F32)),
        in_specs=[hbm, hbm, vmem, smem, hbm, hbm, hbm, hbm, hbm, smem, smem],
        out_specs=(vmem, smem),
        scratch_shapes=[
            pltpu.VMEM((18, 4, 144, 128), F32),
            pltpu.VMEM((2, 2, 4, 1024, 1024), BF16),
            pltpu.VMEM((2, 1024, 1024), BF16),
            pltpu.VMEM((16, 16, 8, 512), F32),
            pltpu.VMEM((16, 4, 128, 128), jnp.int32),
            pltpu.VMEM((256, 1024), BF16),
            pltpu.VMEM((256, 1024), F32),
            pltpu.VMEM((256, 1024), BF16),
            pltpu.VMEM((4, 256, 1024), BF16),
            pltpu.VMEM((2, 256, 128), F32),
            pltpu.VMEM((512, 512), F32),
            pltpu.VMEM((1024, 512), BF16),
            pltpu.VMEM((96, 512), F32),
            pltpu.VMEM((1024, 256), BF16),
            pltpu.VMEM((2, 1024), F32),
            pltpu.VMEM((2, 4, 16, 128), F32),
            pltpu.VMEM((256, 256), F32),
            pltpu.VMEM((8, 16, 128), F32),
            pltpu.VMEM((16, 16, 128), F32),
            dma((4, 4)), dma((4, 4)), dma((2, 2)), dma((2, 2)), dma((4, 4)), dma((4,)),
            dma((7, 2)), dma((7, 2)), dma((7, 2)), dma((7, 2)),
            dma((7, 2)), dma((7, 2)), dma((7, 2)), dma((7, 2)),
            dma((7, 3, 2)), dma((7, 3, 2)), dma((7, 3, 2)), dma((7, 3, 2)),
            dma((7, 3)), dma((7, 3)),
            dma((23,)), dma((23,)),
            dma((13,)),
        ],
        compiler_params=pltpu.CompilerParams(
            collective_id=0, has_side_effects=True, vmem_limit_bytes=60 * 1024 * 1024
        ),
    )(
        volume, labels, patch_list, stem_kernel, embed_weight, norm_gain,
        up_weight, down_weight, head_weight, skip_weight, class_bias,
    )


def solution(mesh):
    placed = (
        P("gz", "gy", None),
        P("gz", "gy", None),
        P("gz", "gy", None),
        P(),
        P(),
        P(),
        P(None, None, "gy"),
        P(None, "gy", None),
        P(),
        P(),
        P(),
    )
    return jax.shard_map(
        per_device,
        mesh=mesh,
        in_specs=placed,
        out_specs=(P("gz", "gy", None, None), P()),
        check_vma=False,
    )
```
